32 devices in a mesh: node: 8 (over z, y), local: 4 (over x, core).
Axes of the slice: x: 2, y: 2, z: 4, core: 2. Of those that a mesh axis runs over, the one named last changes fastest.
Arguments:
- hidden_in: bfloat16 [1024, 7168], P('node', 'local'), may hold values from -6 to 6
- out_grad: bfloat16 [1024, 7168], P('node', 'local'), may hold values from -0.59765625 to 0.59765625
- expert_ids: int32 [1024, 6], P('node'), may hold values from 0 to 15, as said below
- group_ids: int32 [1024, 4], P('node'), may hold values from 0 to 7, as said below
- expert_slot: int32 [1024, 6], P('node'), may hold values from 0 to 63, as said below
- gate_weight: bfloat16 [1024, 6], P('node'), may hold values from 0.099609375 to 1
- w_gate: bfloat16 [16, 7168, 1024], P('node', 'local'), may hold values from -0.0625 to 0.0625
- w_up: bfloat16 [16, 7168, 1024], P('node', 'local'), may hold values from -0.0625 to 0.0625
- w_down: bfloat16 [16, 1024, 7168], P('node', None, 'local'), may hold values from -0.1875 to 0.1875
Outputs:
- grad_input: bfloat16 [1024, 7168], P('node', 'local')
- grad_gate: bfloat16 [1024, 6], P('node')
- grad_w_gate: bfloat16 [16, 7168, 1024], P('node', 'local')
- grad_w_up: bfloat16 [16, 7168, 1024], P('node', 'local')
- grad_w_down: bfloat16 [16, 1024, 7168], P('node', None, 'local')
The draws below stay inside these ranges and needn't reach their ends.
Inputs may be any that keep to these rules, and one draw needn't show every extreme that they name: `expert_ids`: each row names 6 different experts; expert e sits on node e // 2. A row names both experts of two of its nodes and one expert of each of the other two, and only experts on the nodes that group_ids names in the same row. `group_ids`: the 4 nodes of a row differ. In each aligned block of 128 rows every node is named by exactly 64 rows. `expert_slot`: within each aligned block of 128 rows, the entries that name one expert carry the slots 0, 1, 2, ... in row order; some experts fill all 64 slots in every block.
All inputs are finite; a program needn't handle non-finite values.
Results may differ from the reference program's by a relative error of at most 0.008.
Values may be sent and summed in bfloat16 or wider, within the bound.
No kernel may reach another device: no remote copies, remote signals or barrier semaphores. Data moves between devices by JAX's collectives and lax.ppermute only.
A program may use at most 192 MiB of HBM per device.

```python
import jax
import jax.numpy as jnp
from jax import lax

D = 7168
HID = 1024
EXP_NODE = 2
TOPK = 6
GROUPS = 4
TOK_NODE = 128
TOKENS = 1024
EXPERTS = 16
CAP = 64


def draw_order(order_key):
    return jax.random.permutation(order_key, TOK_NODE)


def routing(base_key):
    blocks = TOKENS // TOK_NODE
    capacity = 4 * TOK_NODE // blocks
    key_perm, key_turn, key_pair, key_bits = jax.random.split(base_key, 4)
    orders = jax.vmap(draw_order)(jax.random.split(key_perm, blocks * GROUPS))
    places = jnp.argsort(orders, axis=1).astype(jnp.int32).reshape(blocks, GROUPS, TOK_NODE)
    rotation = jax.random.randint(key_turn, (blocks, 1, 1), 0, 4)
    lane_ids = jnp.arange(GROUPS, dtype=jnp.int32)[None, :, None]
    lane_nodes = 4 * (places // capacity) + (lane_ids + rotation) % 4
    group_ids = jnp.transpose(lane_nodes, (0, 2, 1)).reshape(TOKENS, GROUPS).astype(jnp.int32)
    paired = jax.random.randint(key_pair, (TOKENS,), 1, 4)
    expert_bits = jax.random.randint(key_bits, (TOKENS, 2), 0, 2)
    other_first = jnp.where(paired == 1, 2, 1)
    other_second = jnp.where(paired == 3, 2, 3)
    lead_node = group_ids[:, 0]
    pair_node = jnp.take_along_axis(group_ids, paired[:, None], axis=1)[:, 0]
    single_first = jnp.take_along_axis(group_ids, other_first[:, None], axis=1)[:, 0]
    single_second = jnp.take_along_axis(group_ids, other_second[:, None], axis=1)[:, 0]
    experts = jnp.stack([EXP_NODE * lead_node, EXP_NODE * lead_node + 1, EXP_NODE * pair_node, EXP_NODE * pair_node + 1, EXP_NODE * single_first + expert_bits[:, 0], EXP_NODE * single_second + expert_bits[:, 1]], axis=1).astype(jnp.int32)
    hot_counts = jnp.sum((experts[:, :, None] == jnp.arange(EXPERTS, dtype=jnp.int32)[None, None, :]).astype(jnp.int32), axis=1)
    hot_counts = hot_counts.reshape(blocks, TOK_NODE, EXPERTS)
    before = (jnp.cumsum(hot_counts, axis=1) - hot_counts).reshape(TOKENS, EXPERTS)
    slot_ids = jnp.take_along_axis(before, experts, axis=1).astype(jnp.int32)
    return (experts, group_ids, slot_ids)


def draw_expert_ids(key, part):
    return routing(key)[0]


def draw_group_ids(key, part):
    return routing(key)[1]


def draw_expert_slot(key, part):
    return routing(key)[2]


def block_scale(own_key, extent, cuts, low, top_value):
    gain = 1.0
    for position, shards_of in cuts:
        draws = jax.random.uniform(jax.random.fold_in(jax.random.fold_in(own_key, 6), position), (shards_of,), jnp.float32, low / len(cuts), top_value / len(cuts))
        gain = gain * jnp.repeat(jnp.exp(draws), extent[position] // shards_of).reshape((-1,) + (1,) * (len(extent) - 1 - position))
    return gain


def gaussian(own_key, dims, scale, reach, pieces=(), held_as=jnp.bfloat16):
    values = scale * jax.random.normal(own_key, dims, jnp.float32)
    if pieces:
        values = values * block_scale(own_key, dims, pieces, -0.22, 0.18)
    return jnp.clip(values, -reach, reach).astype(held_as)


def setup_inputs(seed: int = 0) -> dict:
    keys = jax.random.split(jax.random.key(seed), 10)
    hidden_in = gaussian(keys[0], (TOKENS, D), 1.0, 6.0, ((0, 8), (1, 4)))
    out_grad = gaussian(keys[1], (TOKENS, D), 0.1, 0.59765625, ((0, 8), (1, 4)))
    expert_ids = draw_expert_ids(jax.random.fold_in(keys[9], 71), 0)
    group_ids = draw_group_ids(jax.random.fold_in(keys[9], 71), 0)
    expert_slot = draw_expert_slot(jax.random.fold_in(keys[9], 71), 0)
    gate_weight = jnp.clip(0.099609375 + 0.9003906 * jax.random.uniform(keys[5], (TOKENS, TOPK), jnp.float32) ** block_scale(keys[5], (TOKENS, TOPK), ((0, 8),), -0.2, 0.2), 0.099609375, 1.0).astype(jnp.bfloat16)
    w_gate = gaussian(keys[6], (EXPERTS, D, HID), D ** -0.5, 0.0625, ((0, 8), (1, 4)))
    w_up = gaussian(keys[7], (EXPERTS, D, HID), D ** -0.5, 0.0625, ((0, 8), (1, 4)))
    w_down = gaussian(keys[8], (EXPERTS, HID, D), HID ** -0.5, 0.1875, ((0, 8), (2, 4)))
    return {"hidden_in": hidden_in, "out_grad": out_grad, "expert_ids": expert_ids, "group_ids": group_ids, "expert_slot": expert_slot, "gate_weight": gate_weight, "w_gate": w_gate, "w_up": w_up, "w_down": w_down}


def expert_backward(rows_in, rows_grad, rows_gate, gate_mat, up_mat, down_mat):
    pre_gate = jnp.dot(rows_in, gate_mat, preferred_element_type=jnp.float32)
    pre_up = jnp.dot(rows_in, up_mat, preferred_element_type=jnp.float32)
    back_proj = jnp.dot(rows_grad, down_mat.T, preferred_element_type=jnp.float32)
    gate_scale = rows_gate.astype(jnp.float32)[:, None]
    sigmoid_gate = jax.nn.sigmoid(pre_gate)
    silu_gate = pre_gate * sigmoid_gate
    hidden = (silu_gate * pre_up).astype(jnp.bfloat16)
    grad_hidden = gate_scale * back_proj
    grad_gate_pre = (grad_hidden * pre_up * sigmoid_gate * (1.0 + pre_gate * (1.0 - sigmoid_gate))).astype(jnp.bfloat16)
    grad_up_pre = (grad_hidden * silu_gate).astype(jnp.bfloat16)
    gate_term = jnp.sum(hidden.astype(jnp.float32) * back_proj, axis=1).astype(jnp.bfloat16)
    scaled_grad = (gate_scale * rows_grad.astype(jnp.float32)).astype(jnp.bfloat16)
    input_part = jnp.dot(grad_gate_pre, gate_mat.T, preferred_element_type=jnp.float32) + jnp.dot(grad_up_pre, up_mat.T, preferred_element_type=jnp.float32)
    grad_gate_mat = jnp.dot(rows_in.T, grad_gate_pre, preferred_element_type=jnp.float32).astype(jnp.bfloat16)
    grad_up_mat = jnp.dot(rows_in.T, grad_up_pre, preferred_element_type=jnp.float32).astype(jnp.bfloat16)
    grad_down_mat = jnp.dot(hidden.T, scaled_grad, preferred_element_type=jnp.float32).astype(jnp.bfloat16)
    return input_part, gate_term, grad_gate_mat, grad_up_mat, grad_down_mat


def reference(hidden_in, out_grad, expert_ids, group_ids, expert_slot, gate_weight, w_gate, w_up, w_down):
    blocks = TOKENS // TOK_NODE
    row_total = blocks * CAP
    token_index = jnp.arange(TOKENS, dtype=jnp.int32)
    source = token_index // TOK_NODE
    flat_index = ((expert_ids * blocks + source[:, None]) * CAP + expert_slot).astype(jnp.int32)
    owners = jnp.full((EXPERTS * row_total,), TOKENS, dtype=jnp.int32)
    owners = owners.at[flat_index.reshape(-1)].set(jnp.broadcast_to(token_index[:, None], flat_index.shape).reshape(-1))
    gate_rows = jnp.zeros((EXPERTS * row_total,), gate_weight.dtype).at[flat_index.reshape(-1)].set(gate_weight.reshape(-1))
    padded_in = jnp.concatenate([hidden_in, jnp.zeros((1, D), hidden_in.dtype)], axis=0)
    padded_grad = jnp.concatenate([out_grad, jnp.zeros((1, D), out_grad.dtype)], axis=0)

    def per_expert(operands):
        owner_rows, gate_part, gate_mat, up_mat, down_mat = operands
        return expert_backward(padded_in[owner_rows], padded_grad[owner_rows], gate_part, gate_mat, up_mat, down_mat)

    input_parts, gate_terms, grad_w_gate, grad_w_up, grad_w_down = lax.map(
        per_expert, (owners.reshape(EXPERTS, row_total), gate_rows.reshape(EXPERTS, row_total), w_gate, w_up, w_down))
    grad_gate = gate_terms.reshape(-1)[flat_index]
    part_table = input_parts.reshape(EXPERTS, blocks, CAP, D)
    node_of = (expert_ids // EXP_NODE).astype(jnp.int32)

    def combine(operands):
        block_index, block_ids, block_slots, block_nodes, block_groups = operands
        block_table = lax.dynamic_index_in_dim(part_table, block_index, 1, keepdims=False).reshape(EXPERTS * CAP, D)
        picked = block_table[(block_ids * CAP + block_slots).astype(jnp.int32)]
        matches = block_nodes[:, None, :] == block_groups[:, :, None]
        node_part = jnp.sum(jnp.where(matches[:, :, :, None], picked[:, None, :, :], jnp.zeros((), picked.dtype)), axis=2)
        rounded = lax.optimization_barrier(node_part.astype(jnp.bfloat16))
        return jnp.sum(rounded.astype(jnp.float32), axis=1).astype(jnp.bfloat16)

    grad_input = lax.map(combine, (
        jnp.arange(blocks, dtype=jnp.int32),
        expert_ids.reshape(blocks, TOK_NODE, TOPK),
        expert_slot.reshape(blocks, TOK_NODE, TOPK),
        node_of.reshape(blocks, TOK_NODE, TOPK),
        group_ids.reshape(blocks, TOK_NODE, GROUPS))).reshape(TOKENS, D)
    return grad_input, grad_gate, grad_w_gate, grad_w_up, grad_w_down
```

```python
import functools

import jax
import jax.numpy as jnp
from jax import lax
from jax.experimental import pallas as pl
from jax.experimental.pallas import tpu as pltpu
from jax.sharding import PartitionSpec as P

BF = jnp.bfloat16
F32 = jnp.float32
CHUNKS = 2
VMEM = 40 * 1024 * 1024


def params(limit=VMEM):
    return pltpu.CompilerParams(vmem_limit_bytes=limit)


def cost(flops, moved):
    return pl.CostEstimate(flops=int(flops), bytes_accessed=int(moved), transcendentals=0)


def tile_of(size, want):
    tile = min(size, want)
    while size % tile:
        tile //= 2
    return tile


def dot_nn(left, right):
    return lax.dot_general(left, right, (((1,), (0,)), ((), ())), preferred_element_type=F32)


def dot_nt(left, right):
    return lax.dot_general(left, right, (((1,), (1,)), ((), ())), preferred_element_type=F32)


def proj_kernel(transposed, count, *refs):
    rows_ref, mats, own_ref, other_ref = refs[0], refs[1 : 1 + count], refs[-2], refs[-1]
    blocks, _, half, width = rows_ref.shape
    rows = rows_ref[...].reshape(blocks * 2 * half, width)
    for index, mat_ref in enumerate(mats):
        out = dot_nt(rows, mat_ref[0]) if transposed else dot_nn(rows, mat_ref[0])
        out = out.reshape(blocks, 2, half, out.shape[-1])
        own_ref[0, index] = out[:, 0].reshape(blocks * half, out.shape[-1])
        other_ref[0, index] = out[:, 1].reshape(blocks * half, out.shape[-1])


def project(rows, mats, transposed):
    blocks, _, half, width = rows.shape
    experts = mats[0].shape[0]
    hid = mats[0].shape[1] if transposed else mats[0].shape[2]
    count, kept = len(mats), blocks * half
    tile = tile_of(hid, 256)
    if transposed:
        mat_spec = pl.BlockSpec((1, tile, width), lambda e, j: (e, j, 0))
    else:
        mat_spec = pl.BlockSpec((1, width, tile), lambda e, j: (e, 0, j))
    out_spec = pl.BlockSpec((1, count, kept, tile), lambda e, j: (e, 0, 0, j))
    shape = jax.ShapeDtypeStruct((experts, count, kept, hid), F32)
    return pl.pallas_call(
        functools.partial(proj_kernel, transposed, count),
        grid=(experts, hid // tile),
        in_specs=[pl.BlockSpec(rows.shape, lambda e, j: (0, 0, 0, 0))] + [mat_spec] * count,
        out_specs=[out_spec, out_spec],
        out_shape=[shape, shape],
        compiler_params=params(),
        cost_estimate=cost(
            4 * kept * width * hid * experts * count, 2 * width * hid * experts * count
        ),
        name="project",
    )(rows, *mats)


def act_kernel(in_a, in_b, grad_a, grad_b, gate_ref, acts_ref, term_ref):
    pre_gate = in_a[0, 0].astype(F32) + in_b[0, 0].astype(F32)
    pre_up = in_a[0, 1].astype(F32) + in_b[0, 1].astype(F32)
    back = grad_a[0, 0].astype(F32) + grad_b[0, 0].astype(F32)
    scale = gate_ref[0]
    sig = jax.nn.sigmoid(pre_gate)
    silu = pre_gate * sig
    hidden = (silu * pre_up).astype(BF)
    grad_hidden = scale * back
    acts_ref[0, 0] = (grad_hidden * pre_up * sig * (1.0 + pre_gate * (1.0 - sig))).astype(BF)
    acts_ref[0, 1] = (grad_hidden * silu).astype(BF)
    acts_ref[0, 2] = hidden
    term_ref[0] = jnp.sum(hidden.astype(F32) * back, axis=1, keepdims=True)


def activate(in_a, in_b, grad_a, grad_b, gates):
    experts, _, kept, hid = in_a.shape
    tile = tile_of(kept, 64)
    two = pl.BlockSpec((1, 2, tile, hid), lambda e, r: (e, 0, r, 0))
    one = pl.BlockSpec((1, 1, tile, hid), lambda e, r: (e, 0, r, 0))
    col = pl.BlockSpec((1, tile, 1), lambda e, r: (e, r, 0))
    return pl.pallas_call(
        act_kernel,
        grid=(experts, kept // tile),
        in_specs=[two, two, one, one, col],
        out_specs=[pl.BlockSpec((1, 3, tile, hid), lambda e, r: (e, 0, r, 0)), col],
        out_shape=[
            jax.ShapeDtypeStruct((experts, 3, kept, hid), BF),
            jax.ShapeDtypeStruct((experts, kept, 1), F32),
        ],
        compiler_params=params(),
        cost_estimate=cost(30 * experts * kept * hid, 18 * experts * kept * hid),
        name="activate",
    )(in_a, in_b, grad_a, grad_b, gates)


def back_kernel(own_ref, other_ref, gate_ref, up_ref, out_ref):
    experts, _, kept, hid = own_ref.shape
    blocks, _, half, tile = out_ref.shape
    for place, acts_ref in enumerate((own_ref, other_ref)):
        total = jnp.zeros((kept, tile), F32)
        for e in range(experts):
            total = total + dot_nt(acts_ref[e, 0], gate_ref[e])
            total = total + dot_nt(acts_ref[e, 1], up_ref[e])
        out_ref[:, place] = total.astype(BF).reshape(blocks, half, tile)


def back(own, other, w_gate, w_up, blocks):
    experts, _, kept, hid = own.shape
    width = w_gate.shape[1]
    tile = tile_of(width, 256)
    acts = pl.BlockSpec((experts, 2, kept, hid), lambda j: (0, 0, 0, 0))
    mat = pl.BlockSpec((experts, tile, hid), lambda j: (0, j, 0))
    half = kept // blocks
    return pl.pallas_call(
        back_kernel,
        grid=(width // tile,),
        in_specs=[acts, acts, mat, mat],
        out_specs=pl.BlockSpec((blocks, 2, half, tile), lambda j: (0, 0, 0, j)),
        out_shape=jax.ShapeDtypeStruct((blocks, 2, half, width), BF),
        compiler_params=params(),
        cost_estimate=cost(8 * kept * width * hid * experts, 4 * width * hid * experts),
        name="back",
    )(own, other, w_gate, w_up)


def grads_kernel(chunks, *refs):
    ins, grads = refs[:chunks], refs[chunks : 2 * chunks]
    acts = refs[2 * chunks : 4 * chunks]
    gate_ref, out_gate, out_up, out_down, hidden_t = refs[4 * chunks :]
    kept = acts[0].shape[2]

    def pieces(which):
        return jnp.concatenate([ref[0, which] for ref in acts], axis=0)

    @pl.when(pl.program_id(1) == 0)
    def _():
        hidden_t[...] = pieces(2).T

    def rows_of(refs_in):
        out = []
        for ref in refs_in:
            for place in range(2):
                out.append(ref[:, place].reshape(kept, ref.shape[-1]))
        return jnp.concatenate(out, axis=0)

    rows_t = rows_of(ins).T
    out_gate[0] = dot_nn(rows_t, pieces(0)).astype(BF)
    out_up[0] = dot_nn(rows_t, pieces(1)).astype(BF)
    scaled = (gate_ref[0] * rows_of(grads).astype(F32)).astype(BF)
    out_down[0] = dot_nn(hidden_t[...], scaled).astype(BF)


def weight_grads(ins, grads, acts, gates):
    chunks = len(ins)
    blocks, _, half, width = ins[0].shape
    experts, _, kept, hid = acts[0].shape
    rows = 2 * kept * chunks
    tile = tile_of(width, 256)
    row_spec = pl.BlockSpec((blocks, 2, half, tile), lambda e, j: (0, 0, 0, j))
    act_spec = pl.BlockSpec((1, 3, kept, hid), lambda e, j: (e, 0, 0, 0))
    wide = pl.BlockSpec((1, tile, hid), lambda e, j: (e, j, 0))
    down = pl.BlockSpec((1, hid, tile), lambda e, j: (e, 0, j))
    wide_shape = jax.ShapeDtypeStruct((experts, width, hid), BF)
    return pl.pallas_call(
        functools.partial(grads_kernel, chunks),
        grid=(experts, width // tile),
        in_specs=[row_spec] * (2 * chunks)
        + [act_spec] * (2 * chunks)
        + [pl.BlockSpec((1, rows, 1), lambda e, j: (e, 0, 0))],
        out_specs=[wide, wide, down],
        out_shape=[wide_shape, wide_shape, jax.ShapeDtypeStruct((experts, hid, width), BF)],
        scratch_shapes=[pltpu.VMEM((hid, rows), BF)],
        compiler_params=params(),
        cost_estimate=cost(6 * rows * width * hid * experts, 6 * width * hid * experts),
        name="weight_grads",
    )(*ins, *grads, *acts, gates)


def local(
    hidden_in, out_grad, expert_ids, group_ids, expert_slot, gate_weight, w_gate, w_up, w_down
):
    nodes = lax.axis_size("node")
    shares = lax.axis_size("local")
    tokens, width = hidden_in.shape
    experts = w_gate.shape[0]
    capacity = 4 * tokens // nodes
    size = capacity // CHUNKS
    half = size // 2
    kept = nodes * half
    core = lax.axis_index("local") % 2

    def swap(value, step):
        return lax.ppermute(value, "local", [(i, i ^ step) for i in range(shares)])

    def spread(value):
        return lax.all_to_all(value, "node", split_axis=0, concat_axis=0, tiled=True)

    node_iota = lax.broadcasted_iota(jnp.int32, (nodes, tokens), 0)
    groups_t = group_ids.T
    member = jnp.zeros((nodes, tokens), jnp.bool_)
    for index in range(group_ids.shape[1]):
        member = member | (groups_t[index][None, :] == node_iota)
    earlier = lax.broadcasted_iota(jnp.int32, (tokens, tokens), 0) < lax.broadcasted_iota(
        jnp.int32, (tokens, tokens), 1
    )
    rank = dot_nn(member.astype(BF), earlier.astype(BF)).astype(jnp.int32)
    place = jnp.where(member, rank ^ (core * half), -1)
    hot = (
        place[:, None, :] == lax.broadcasted_iota(jnp.int32, (nodes, capacity, tokens), 1)
    ).astype(BF)
    hot_parts = [
        hot[:, index * size : (index + 1) * size].reshape(nodes * size, tokens)
        for index in range(CHUNKS)
    ]
    expert_iota = lax.broadcasted_iota(jnp.int32, (nodes * experts, tokens), 0)
    ids_t, gate_t = expert_ids.T, gate_weight.T
    table = jnp.zeros((nodes * experts, tokens), BF)
    for index in range(expert_ids.shape[1]):
        table = jnp.where(ids_t[index][None, :] == expert_iota, gate_t[index][None, :], table)
    send_gate = jnp.einsum(
        "njt,npt->njp",
        table.reshape(nodes, experts, tokens),
        hot,
        preferred_element_type=F32,
    ).astype(BF)
    recv_gate = spread(send_gate)

    def pack(values, index):
        sent = dot_nn(hot_parts[index], values).astype(BF)
        return spread(sent.reshape(nodes, size, width)).reshape(nodes, 2, half, width)

    rows_in = [pack(hidden_in, index) for index in range(CHUNKS)]
    rows_grad = [pack(out_grad, index) for index in range(CHUNKS)]
    gates = (
        recv_gate.astype(F32)
        .reshape(nodes, experts, CHUNKS, 2, half)
        .transpose(1, 2, 3, 0, 4)
        .reshape(experts, CHUNKS, 2, kept)
    )

    def summed(rows, mats, transposed):
        own, other = project(rows, mats, transposed)
        mine = (own + swap(other, 1)).astype(BF)
        step = 2
        while 2 * step < shares:
            mine = (mine.astype(F32) + swap(mine, step).astype(F32)).astype(BF)
            step *= 2
        return mine, swap(mine, step)

    sums_in = [summed(rows, (w_gate, w_up), False) for rows in rows_in]
    sums_grad = [summed(rows, (w_down,), True) for rows in rows_grad]

    acts, terms, returned = [], [], []
    for index in range(CHUNKS):
        own, term = activate(
            *sums_in[index], *sums_grad[index], gates[:, index, 0][:, :, None]
        )
        other = swap(own, 1)
        acts += [own, other]
        mine = term[:, :, 0].astype(BF)
        terms.append(jnp.stack([mine, swap(mine, 1)], axis=1))
        sent = back(own, other, w_gate, w_up, nodes)
        returned.append(spread(sent.reshape(nodes, size, width)).reshape(nodes * size, width))

    grad_w_gate, grad_w_up, grad_w_down = weight_grads(
        rows_in, rows_grad, acts, gates.reshape(experts, nodes * capacity)[:, :, None]
    )

    total = jnp.zeros((tokens, width), F32)
    for index in range(CHUNKS):
        total = total + lax.dot_general(
            hot_parts[index],
            returned[index],
            (((0,), (0,)), ((), ())),
            preferred_element_type=F32,
        )
    grad_input = total.astype(BF)

    all_terms = (
        jnp.stack(terms, axis=1)
        .reshape(experts, CHUNKS, 2, nodes, half)
        .transpose(3, 0, 1, 2, 4)
        .reshape(nodes, experts, capacity)
    )
    home = jnp.einsum("njp,npt->njt", spread(all_terms), hot, preferred_element_type=F32)
    home = home.reshape(nodes * experts, tokens)
    picked = [
        jnp.sum(jnp.where(ids_t[index][None, :] == expert_iota, home, 0.0), axis=0)
        for index in range(expert_ids.shape[1])
    ]
    grad_gate = jnp.stack(picked, axis=1).astype(BF)
    return (grad_input, grad_gate, grad_w_gate, grad_w_up, grad_w_down)


def solution(mesh):
    return jax.shard_map(
        local,
        mesh=mesh,
        in_specs=(
            P("node", "local"),
            P("node", "local"),
            P("node", None),
            P("node", None),
            P("node", None),
            P("node", None),
            P("node", "local", None),
            P("node", "local", None),
            P("node", None, "local"),
        ),
        out_specs=(
            P("node", "local"),
            P("node", None),
            P("node", "local", None),
            P("node", "local", None),
            P("node", None, "local"),
        ),
        check_vma=False,
    )
```

```python
import functools

import jax
import jax.numpy as jnp
from jax import lax
from jax.experimental import pallas as pl
from jax.experimental.pallas import tpu as pltpu
from jax.sharding import PartitionSpec as P

BF = jnp.bfloat16
F32 = jnp.float32
MIB = 1024 * 1024
LANES = 128
IN_VMEM = pl.BlockSpec(memory_space=pltpu.VMEM)
IN_SMEM = pl.BlockSpec(memory_space=pltpu.SMEM)
IN_HBM = pl.BlockSpec(memory_space=pltpu.HBM)
ANYWHERE = pl.BlockSpec(memory_space=pl.ANY)
MARK = pl.CostEstimate(flops=4000000000, bytes_accessed=1024, transcendentals=0)
CHEAP = pl.CostEstimate(flops=1024, bytes_accessed=1024, transcendentals=0)


def params(mib):
    return pltpu.CompilerParams(vmem_limit_bytes=mib * MIB)


def call(kernel, deps, operands, in_specs, **settings):
    count, extra = len(operands), len(deps)

    def body(*refs):
        kernel(*refs[:count], *refs[count + extra :])

    return pl.pallas_call(body, in_specs=list(in_specs) + [ANYWHERE] * extra, **settings)(
        *operands, *deps
    )


def tile_of(size, want):
    tile = min(size, want)
    while size % tile:
        tile //= 2
    return tile


def dot_nn(left, right):
    return lax.dot_general(left, right, (((1,), (0,)), ((), ())), preferred_element_type=F32)


def dot_nt(left, right):
    return lax.dot_general(left, right, (((1,), (1,)), ((), ())), preferred_element_type=F32)


def resident(array):
    return pltpu.with_memory_space_constraint(array, pltpu.VMEM)


def remote(array):
    return pltpu.with_memory_space_constraint(array, pltpu.HBM)


def fetch(pairs, sems):
    copies = [pltpu.make_async_copy(src, dst, sems.at[i]) for i, (src, dst) in enumerate(pairs)]
    for copy in copies:
        copy.start()
    for copy in copies:
        copy.wait()


def join(pieces):
    return pieces[0] if len(pieces) == 1 else jnp.concatenate(pieces, axis=0)


def load_kernel(count, *refs):
    fetch(list(zip(refs[:count], refs[count : 2 * count])), refs[2 * count])


def load(mats, deps):
    count = len(mats)
    return call(
        functools.partial(load_kernel, count),
        deps,
        [remote(mat) for mat in mats],
        [IN_HBM] * count,
        out_specs=[IN_VMEM] * count,
        out_shape=[pltpu.VMEM(mat.shape, mat.dtype) for mat in mats],
        scratch_shapes=[pltpu.SemaphoreType.DMA((count,))],
        compiler_params=params(1),
        cost_estimate=CHEAP,
        name="load",
    )


def hot_block(place_ref, index, size):
    tokens = place_ref.shape[1]
    row = lax.broadcasted_iota(jnp.int32, (size, tokens), 0)
    return jnp.where(place_ref[index : index + 1, :] == row, 1.0, 0.0).astype(BF)


def route_kernel(where_ref, groups_ref, ids_ref, gates_ref, place_ref, table_ref):
    me, flip = where_ref[0], where_ref[1]
    tokens = place_ref.shape[1]
    peers = me ^ lax.broadcasted_iota(jnp.int32, place_ref.shape, 0)
    member = jnp.zeros(place_ref.shape, F32)
    for index in range(groups_ref.shape[0]):
        member = jnp.where(groups_ref[index : index + 1, :] == peers, 1.0, member)
    earlier = jnp.where(
        lax.broadcasted_iota(jnp.int32, (tokens, tokens), 0)
        < lax.broadcasted_iota(jnp.int32, (tokens, tokens), 1),
        1.0,
        0.0,
    ).astype(BF)
    rank = dot_nn(member.astype(BF), earlier).astype(jnp.int32)
    place_ref[...] = jnp.where(member > 0.0, rank ^ flip, -1)
    expert = lax.broadcasted_iota(jnp.int32, (LANES, tokens), 0)
    table = jnp.zeros((LANES, tokens), F32)
    for index in range(ids_ref.shape[0]):
        gate = gates_ref[index : index + 1, :].astype(F32)
        table = jnp.where(ids_ref[index : index + 1, :] == expert, gate, table)
    table_ref[...] = table.astype(BF)


def route(where, groups_t, ids_t, gates_t, nodes):
    tokens = ids_t.shape[1]
    return pl.pallas_call(
        route_kernel,
        in_specs=[IN_SMEM] + [IN_VMEM] * 3,
        out_specs=[IN_VMEM] * 2,
        out_shape=[
            jax.ShapeDtypeStruct((nodes, tokens), jnp.int32),
            jax.ShapeDtypeStruct((LANES, tokens), BF),
        ],
        compiler_params=params(4),
        cost_estimate=CHEAP,
        name="route",
    )(where, groups_t, ids_t, gates_t)


def pack_kernel(masks, place_ref, in_ref, grad_ref, table_ref, *outs):
    width = in_ref.shape[1]
    for mask, out in zip(masks, outs):
        hot = hot_block(place_ref, mask, out.shape[0])
        out[:, :width] = dot_nn(hot, in_ref[...]).astype(BF)
        out[:, width : 2 * width] = dot_nn(hot, grad_ref[...]).astype(BF)
        out[:, 2 * width :] = dot_nt(hot, table_ref[...]).astype(BF)


def pack(place, hidden_in, out_grad, table, masks, size, deps):
    block = jax.ShapeDtypeStruct((size, 2 * hidden_in.shape[1] + LANES), BF)
    return call(
        functools.partial(pack_kernel, list(masks)),
        deps,
        [place, hidden_in, out_grad, table],
        [IN_VMEM] * 4,
        out_specs=[IN_VMEM] * len(masks),
        out_shape=[block] * len(masks),
        compiler_params=params(8),
        cost_estimate=CHEAP,
        name="pack",
    )


def unpack_kernel(place_ref, ids_ref, *refs):
    blocks, (grad_ref, gate_ref, rows, sems) = refs[:-4], refs[-4:]
    size = blocks[0].shape[0]
    tokens, width = grad_ref.shape
    pieces = [rows.at[index * size : (index + 1) * size] for index in range(len(blocks))]
    fetch(list(zip(blocks, pieces)), sems)
    hot = join([hot_block(place_ref, index, size) for index in range(len(blocks))])
    contract = (((0,), (0,)), ((), ()))
    grad_ref[...] = lax.dot_general(
        hot, rows[:, :width], contract, preferred_element_type=F32
    ).astype(BF)
    terms = lax.dot_general(rows[:, width:], hot, contract, preferred_element_type=F32)
    expert = lax.broadcasted_iota(jnp.int32, (LANES, tokens), 0)
    for index in range(ids_ref.shape[0]):
        chosen = jnp.where(ids_ref[index : index + 1, :] == expert, terms, 0.0)
        gate_ref[index : index + 1, :] = jnp.sum(chosen, axis=0, keepdims=True)


def unpack(place, ids_t, blocks):
    size, wide = blocks[0].shape
    count, tokens = ids_t.shape
    return pl.pallas_call(
        unpack_kernel,
        in_specs=[IN_VMEM] * 2 + [ANYWHERE] * len(blocks),
        out_specs=[IN_VMEM] * 2,
        out_shape=[
            jax.ShapeDtypeStruct((tokens, wide - LANES), BF),
            jax.ShapeDtypeStruct((count, tokens), F32),
        ],
        scratch_shapes=[
            pltpu.VMEM((size * len(blocks), wide), BF),
            pltpu.SemaphoreType.DMA((len(blocks),)),
        ],
        compiler_params=params(12),
        cost_estimate=CHEAP,
        name="unpack",
    )(place, ids_t, *blocks)


def project_kernel(blocks, *refs):
    (gate_ref, up_ref, down_ref), (own_ref, other_ref, rows_ref, sems) = refs[blocks:-4], refs[-4:]
    width = rows_ref.shape[1] // 2
    half = refs[0].shape[0] // 2
    experts, _, kept, hid = own_ref.shape
    pairs = []
    for index, block in enumerate(refs[:blocks]):
        for place in range(2):
            start = place * kept + index * half
            pairs.append(
                (
                    block.at[place * half : (place + 1) * half, : 2 * width],
                    rows_ref.at[start : start + half],
                )
            )
    fetch(pairs, sems)
    rows_in, rows_grad = rows_ref[:, :width], rows_ref[:, width:]
    tile = tile_of(hid, 512)

    def put(e, index, part, value):
        own_ref[e, index, :, part] = value[:kept]
        other_ref[e, index, :, part] = value[kept:]

    for e in range(experts):
        for start in range(0, hid, tile):
            part = slice(start, start + tile)
            put(e, 0, part, dot_nn(rows_in, gate_ref[e, :, part]))
            put(e, 1, part, dot_nn(rows_in, up_ref[e, :, part]))
            put(e, 2, part, dot_nt(rows_grad, down_ref[e, part]))


def project(blocks, w_gate, w_up, w_down, deps):
    experts, width, hid = w_gate.shape
    rows = len(blocks) * blocks[0].shape[0]
    shape = jax.ShapeDtypeStruct((experts, 3, rows // 2, hid), F32)
    return call(
        functools.partial(project_kernel, len(blocks)),
        deps,
        [*blocks, resident(w_gate), resident(w_up), resident(w_down)],
        [ANYWHERE] * len(blocks) + [IN_VMEM] * 3,
        out_specs=[IN_VMEM, IN_VMEM],
        out_shape=[shape, shape],
        scratch_shapes=[
            pltpu.VMEM((rows, 2 * width), BF),
            pltpu.SemaphoreType.DMA((2 * len(blocks),)),
        ],
        compiler_params=params(12),
        cost_estimate=CHEAP,
        name="project",
    )


def add_kernel(own_ref, other_ref, out_ref):
    experts, count, kept, _ = out_ref.shape
    for e in range(experts):
        for index in range(count):

            @pl.loop(0, kept // 16)
            def _(step):
                rows = pl.ds(pl.multiple_of(step * 16, 16), 16)
                total = own_ref[e, index, rows] + other_ref[e, index, rows]
                out_ref[e, index, rows] = total.astype(BF)


def add(own, other, deps):
    return call(
        add_kernel,
        deps,
        [own, other],
        [IN_VMEM] * 2,
        out_specs=IN_VMEM,
        out_shape=jax.ShapeDtypeStruct(own.shape, BF),
        compiler_params=params(12),
        cost_estimate=CHEAP,
        name="add",
    )


def act_kernel(blocks, where_ref, sum_a, sum_b, *refs):
    acts_ref, gates_ref, sems = refs[blocks:]
    experts, _, kept, hid = sum_a.shape
    half = refs[0].shape[0] // 2
    width = refs[0].shape[1] - LANES
    fetch(
        [
            (block.at[:half, width:], gates_ref.at[index * half : (index + 1) * half])
            for index, block in enumerate(refs[:blocks])
        ],
        sems,
    )
    tile = 16
    lane = lax.broadcasted_iota(jnp.int32, (tile, LANES), 1)
    for e in range(experts):
        mine = lane == where_ref[0] * experts + e

        @pl.loop(0, kept // tile)
        def _(step):
            rows = pl.ds(pl.multiple_of(step * tile, tile), tile)
            gates = gates_ref[rows].astype(F32)
            gate = jnp.sum(jnp.where(mine, gates, 0.0), axis=1, keepdims=True)
            pre_gate = sum_a[e, 0, rows].astype(F32) + sum_b[e, 0, rows].astype(F32)
            pre_up = sum_a[e, 1, rows].astype(F32) + sum_b[e, 1, rows].astype(F32)
            back = sum_a[e, 2, rows].astype(F32) + sum_b[e, 2, rows].astype(F32)
            sig = jax.nn.sigmoid(pre_gate)
            silu = pre_gate * sig
            hidden = silu * pre_up
            grad_hidden = gate * back
            slope = sig * (1.0 + pre_gate * (1.0 - sig))
            acts_ref[e, rows, :hid] = (grad_hidden * pre_up * slope).astype(BF)
            acts_ref[e, rows, hid : 2 * hid] = (grad_hidden * silu).astype(BF)
            acts_ref[e, rows, 2 * hid : 3 * hid] = (gate * hidden).astype(BF)
            term = jnp.sum(hidden.astype(BF).astype(F32) * back, axis=1, keepdims=True)
            acts_ref[e, rows, 3 * hid :] = jnp.where(mine, term, 0.0).astype(BF)


def activate(where, sum_a, sum_b, blocks, deps):
    experts, _, kept, hid = sum_a.shape
    return call(
        functools.partial(act_kernel, len(blocks)),
        deps,
        [where, sum_a, sum_b, *blocks],
        [IN_SMEM] + [IN_VMEM] * 2 + [ANYWHERE] * len(blocks),
        out_specs=IN_VMEM,
        out_shape=jax.ShapeDtypeStruct((experts, kept, 3 * hid + LANES), BF),
        scratch_shapes=[
            pltpu.VMEM((kept, LANES), BF),
            pltpu.SemaphoreType.DMA((len(blocks),)),
        ],
        compiler_params=params(8),
        cost_estimate=CHEAP,
        name="activate",
    )


def back_kernel(own_ref, other_ref, gate_ref, up_ref, *refs):
    outs, (acts_ref, terms_ref, sems) = refs[:-3], refs[-3:]
    experts, kept, _ = own_ref.shape
    half = outs[0].shape[0] // 2
    _, width, hid = gate_ref.shape
    pairs = []
    for place, ref in enumerate((own_ref, other_ref)):
        rows = slice(place * kept, (place + 1) * kept)
        pairs.append((ref.at[:, :, : 2 * hid], acts_ref.at[:, rows]))
        pairs.append((ref.at[:, :, 3 * hid :], terms_ref.at[:, rows]))
    fetch(pairs, sems)
    terms = terms_ref[0]
    for e in range(1, experts):
        terms = terms + terms_ref[e]

    def put(value, part):
        for index, out in enumerate(outs):
            out[:half, part] = value[index * half : (index + 1) * half]
            out[half:, part] = value[kept + index * half : kept + (index + 1) * half]

    put(terms, slice(width, width + LANES))
    tile = tile_of(width, 256)
    for start in range(0, width, tile):
        part = slice(start, start + tile)
        total = jnp.zeros((2 * kept, tile), F32)
        for e in range(experts):
            total = total + dot_nt(acts_ref[e, :, :hid], gate_ref[e, part])
            total = total + dot_nt(acts_ref[e, :, hid:], up_ref[e, part])
        put(total.astype(BF), part)


def back(own, other, w_gate, w_up, blocks, deps):
    experts, kept, _ = own.shape
    _, width, hid = w_gate.shape
    shape = jax.ShapeDtypeStruct((2 * kept // blocks, width + LANES), BF)
    return call(
        back_kernel,
        deps,
        [own, other, resident(w_gate), resident(w_up)],
        [ANYWHERE] * 2 + [IN_VMEM] * 2,
        out_specs=[IN_VMEM] * blocks,
        out_shape=[shape] * blocks,
        scratch_shapes=[
            pltpu.VMEM((experts, 2 * kept, 2 * hid), BF),
            pltpu.VMEM((experts, 2 * kept, LANES), BF),
            pltpu.SemaphoreType.DMA((4,)),
        ],
        compiler_params=params(12),
        cost_estimate=CHEAP,
        name="back",
    )


def grads_kernel(groups, *refs):
    blocks = sum(groups)
    acts = refs[2 * blocks : -6]
    out_gate, out_up, out_down, gate_acts, up_acts, hidden_t = refs[-6:]
    hid = gate_acts.shape[1]

    @pl.when(pl.program_id(1) == 0)
    def _():
        first = 0
        for ref in acts:
            rows = slice(first, first + ref.shape[1])
            gate_acts[rows] = ref[0, :, :hid]
            up_acts[rows] = ref[0, :, hid : 2 * hid]
            hidden_t[:, rows] = ref[0, :, 2 * hid : 3 * hid].T
            first += ref.shape[1]

    def rows_of(ins):
        out, first = [], 0
        for count in groups:
            group = ins[first : first + count]
            half = group[0].shape[0] // 2
            out += [ref[:half] for ref in group] + [ref[half:] for ref in group]
            first += count
        return join(out)

    rows_t = rows_of(refs[:blocks]).T
    out_gate[0] = dot_nn(rows_t, gate_acts[...]).astype(BF)
    out_up[0] = dot_nn(rows_t, up_acts[...]).astype(BF)
    out_down[0] = dot_nn(hidden_t[...], rows_of(refs[blocks : 2 * blocks])).astype(BF)


def weight_grads(blocks, acts, groups, deps):
    size, width = blocks[0].shape[0], (blocks[0].shape[1] - LANES) // 2
    experts = acts[0].shape[0]
    hid = (acts[0].shape[2] - LANES) // 3
    rows = size * len(blocks)
    tile = tile_of(width, 256)
    steps = width // tile
    in_spec = pl.BlockSpec((size, tile), lambda e, j: (0, j))
    grad_spec = pl.BlockSpec((size, tile), lambda e, j: (0, steps + j))
    act_specs = [pl.BlockSpec((1,) + act.shape[1:], lambda e, j: (e, 0, 0)) for act in acts]
    wide = pl.BlockSpec((1, tile, hid), lambda e, j: (e, j, 0))
    down = pl.BlockSpec((1, hid, tile), lambda e, j: (e, 0, j))
    wide_shape = jax.ShapeDtypeStruct((experts, width, hid), BF)
    return call(
        functools.partial(grads_kernel, groups),
        deps,
        [*blocks, *blocks, *acts],
        [in_spec] * len(blocks) + [grad_spec] * len(blocks) + act_specs,
        grid=(experts, steps),
        out_specs=[wide, wide, down],
        out_shape=[wide_shape, wide_shape, jax.ShapeDtypeStruct((experts, hid, width), BF)],
        scratch_shapes=[
            pltpu.VMEM((rows, hid), BF),
            pltpu.VMEM((rows, hid), BF),
            pltpu.VMEM((hid, rows), BF),
        ],
        compiler_params=params(32),
        cost_estimate=CHEAP,
        name="weight_grads",
    )


def mark_kernel(out_ref):
    out_ref[...] = jnp.zeros(out_ref.shape, F32)


def mark(deps):
    return call(
        mark_kernel,
        deps,
        [],
        [],
        out_specs=IN_VMEM,
        out_shape=jax.ShapeDtypeStruct((8, LANES), F32),
        compiler_params=params(1),
        cost_estimate=MARK,
        name="mark",
    )


def local(
    hidden_in, out_grad, expert_ids, group_ids, expert_slot, gate_weight, w_gate, w_up, w_down
):
    nodes = lax.axis_size("node")
    shares = lax.axis_size("local")
    capacity = 4 * hidden_in.shape[0] // nodes
    me = lax.axis_index("node")
    core = lax.axis_index("local") % 2
    where = jnp.stack([me, core * (capacity // 2)]).astype(jnp.int32)
    quarter = nodes // 4
    spans = [range(group * quarter, (group + 1) * quarter) for group in range(4)]
    own, near, mid, far = range(4)

    def swap(value, step):
        return lax.ppermute(value, "local", [(i, i ^ step) for i in range(shares)])

    def cross(value, mask):
        if mask == 0:
            return value
        return lax.ppermute(value, "node", [(i, i ^ mask) for i in range(nodes)])

    ids_t = expert_ids.T
    place, table = route(where, group_ids.T, ids_t, gate_weight.T, nodes)
    last = []

    def send_step(group, deps=()):
        blocks = pack(
            place, hidden_in, out_grad, table, spans[group], capacity, [*last, *deps]
        )
        last[:] = [blocks[0]]
        rows[group] = [cross(block, mask) for block, mask in zip(blocks, spans[group])]

    def pause(count):
        for _ in range(count):
            last[:] = [mark(last)]

    def project_step(group):
        mine, other = project(rows[group], v_gate, v_up, v_down, last)
        last[:] = [mine]
        parts[group] = mine, swap(other, 1)

    def sum_step(group):
        pause(24)
        total = add(*parts[group], last)
        last[:] = [total]
        step = 2
        while 2 * step < shares:
            total = (total.astype(F32) + swap(total, step).astype(F32)).astype(BF)
            step *= 2
        sums[group] = total, swap(total, step)

    def act_step(group):
        mine = activate(where, *sums[group], rows[group], last)
        last[:] = [mine]
        acts[group] = mine, swap(mine, 1)

    def back_step(group):
        pause(24)
        blocks = back(*acts[group], v_gate, v_up, len(spans[group]), last)
        last[:] = [blocks[0]]
        for mask, block in zip(spans[group], blocks):
            returned[mask] = cross(block, mask)

    rows, parts, sums, acts = [[None] * 4 for _ in range(4)]
    returned = [None] * nodes
    send_step(own)
    send_step(near)
    send_step(far)
    v_gate, v_up, v_down = load((w_gate, w_up, w_down), last)
    last[:] = [v_gate]
    project_step(own)
    sum_step(own)
    project_step(near)
    send_step(mid, rows[far])
    sum_step(near)
    project_step(far)
    sum_step(far)
    act_step(own)
    back_step(own)
    act_step(near)
    back_step(near)
    project_step(mid)
    sum_step(mid)
    act_step(far)
    back_step(far)
    act_step(mid)
    back_step(mid)

    grad_w_gate, grad_w_up, grad_w_down = weight_grads(
        [block for group in rows for block in group],
        [part for pair in acts for part in pair],
        [len(span) for span in spans],
        last,
    )
    grad_input, grad_gate = unpack(place, ids_t, returned)
    return (grad_input, grad_gate.T.astype(BF), grad_w_gate, grad_w_up, grad_w_down)


def solution(mesh):
    return jax.shard_map(
        local,
        mesh=mesh,
        in_specs=(
            P("node", "local"),
            P("node", "local"),
            P("node", None),
            P("node", None),
            P("node", None),
            P("node", None),
            P("node", "local", None),
            P("node", "local", None),
            P("node", None, "local"),
        ),
        out_specs=(
            P("node", "local"),
            P("node", None),
            P("node", "local", None),
            P("node", "local", None),
            P("node", None, "local"),
        ),
        check_vma=False,
    )
```

```python
import functools

import jax
import jax.numpy as jnp
from jax import lax
from jax.experimental import pallas as pl
from jax.experimental.pallas import tpu as pltpu
from jax.sharding import PartitionSpec as P

BF = jnp.bfloat16
F32 = jnp.float32
MIB = 1024 * 1024
LANES = 128
IN_VMEM = pl.BlockSpec(memory_space=pltpu.VMEM)
IN_SMEM = pl.BlockSpec(memory_space=pltpu.SMEM)
IN_HBM = pl.BlockSpec(memory_space=pltpu.HBM)
ANYWHERE = pl.BlockSpec(memory_space=pl.ANY)
MARK = pl.CostEstimate(flops=4000000000, bytes_accessed=1024, transcendentals=0)
CHEAP = pl.CostEstimate(flops=1024, bytes_accessed=1024, transcendentals=0)


def params(mib):
    return pltpu.CompilerParams(vmem_limit_bytes=mib * MIB)


def call(kernel, deps, operands, in_specs, **settings):
    count, extra = len(operands), len(deps)

    def body(*refs):
        kernel(*refs[:count], *refs[count + extra :])

    return pl.pallas_call(body, in_specs=list(in_specs) + [ANYWHERE] * extra, **settings)(
        *operands, *deps
    )


def tile_of(size, want):
    tile = min(size, want)
    while size % tile:
        tile //= 2
    return tile


def dot_nn(left, right):
    return lax.dot_general(left, right, (((1,), (0,)), ((), ())), preferred_element_type=F32)


def dot_nt(left, right):
    return lax.dot_general(left, right, (((1,), (1,)), ((), ())), preferred_element_type=F32)


def resident(array):
    return pltpu.with_memory_space_constraint(array, pltpu.VMEM)


def remote(array):
    return pltpu.with_memory_space_constraint(array, pltpu.HBM)


def fetch(pairs, sems):
    copies = [pltpu.make_async_copy(src, dst, sems.at[i]) for i, (src, dst) in enumerate(pairs)]
    for copy in copies:
        copy.start()
    for copy in copies:
        copy.wait()


def join(pieces):
    return pieces[0] if len(pieces) == 1 else jnp.concatenate(pieces, axis=0)


def load_kernel(count, *refs):
    fetch(list(zip(refs[:count], refs[count : 2 * count])), refs[2 * count])


def load(mats, deps):
    count = len(mats)
    return call(
        functools.partial(load_kernel, count),
        deps,
        [remote(mat) for mat in mats],
        [IN_HBM] * count,
        out_specs=[IN_VMEM] * count,
        out_shape=[pltpu.VMEM(mat.shape, mat.dtype) for mat in mats],
        scratch_shapes=[pltpu.SemaphoreType.DMA((count,))],
        compiler_params=params(1),
        cost_estimate=CHEAP,
        name="load",
    )


def hot_block(place_ref, index, size):
    tokens = place_ref.shape[1]
    row = lax.broadcasted_iota(jnp.int32, (size, tokens), 0)
    return jnp.where(place_ref[index : index + 1, :] == row, 1.0, 0.0).astype(BF)


def select_rows(experts, where_ref, tokens_ref, outs):
    me, flip = where_ref[0], where_ref[1]
    tokens, width = tokens_ref.shape
    size = outs[0].shape[0]
    lane = lax.broadcasted_iota(jnp.int32, (tokens, LANES), 1)
    holds = (
        lax.broadcasted_iota(jnp.int32, (LANES, LANES), 0) // experts
        == lax.broadcasted_iota(jnp.int32, (LANES, LANES), 1)
    )
    named = jnp.where(tokens_ref[:, width - LANES :].astype(F32) > 0.0, 1.0, 0.0).astype(BF)
    member = dot_nn(named, jnp.where(holds, 1.0, 0.0).astype(BF)) > 0.0
    earlier = (
        lax.broadcasted_iota(jnp.int32, (tokens, tokens), 1)
        < lax.broadcasted_iota(jnp.int32, (tokens, tokens), 0)
    )
    rank = dot_nn(
        jnp.where(earlier, 1.0, 0.0).astype(BF), jnp.where(member, 1.0, 0.0).astype(BF)
    )
    place = jnp.where(member, rank.astype(jnp.int32) ^ flip, -1)
    contract = (((0,), (0,)), ((), ()))
    for index, out in enumerate(outs):
        row = jnp.sum(jnp.where(lane == (me ^ index), place, 0), axis=1, keepdims=True)
        hot = lax.broadcasted_iota(jnp.int32, (tokens, size), 1) == row
        hot = jnp.where(hot, 1.0, 0.0).astype(BF)
        out[...] = lax.dot_general(
            hot, tokens_ref[...], contract, preferred_element_type=F32
        ).astype(BF)


def select_kernel(experts, where_ref, tokens_ref, *outs):
    select_rows(experts, where_ref, tokens_ref, outs)


def select(where, whole, experts, count, size, deps):
    block = jax.ShapeDtypeStruct((size, whole.shape[1]), BF)
    return call(
        functools.partial(select_kernel, experts),
        deps,
        [where, whole],
        [IN_SMEM, IN_VMEM],
        out_specs=[IN_VMEM] * count,
        out_shape=[block] * count,
        compiler_params=params(8),
        cost_estimate=CHEAP,
        name="select",
    )


def route_kernel(experts, where_ref, ids_hbm, gates_hbm, in_hbm, grad_hbm, *refs):
    out_ref, outs = refs[0], refs[1:-3]
    ids_ref, gates_ref, sems = refs[-3:]
    tokens, width = in_hbm.shape
    fetch(
        [
            (ids_hbm, ids_ref),
            (gates_hbm, gates_ref),
            (in_hbm, out_ref.at[:, :width]),
            (grad_hbm, out_ref.at[:, width : 2 * width]),
        ],
        sems,
    )
    expert = lax.broadcasted_iota(jnp.int32, (LANES, tokens), 0)
    table = jnp.zeros((LANES, tokens), F32)
    for index in range(ids_ref.shape[0]):
        gate = gates_ref[index : index + 1, :].astype(F32)
        table = jnp.where(ids_ref[index : index + 1, :] == expert, gate, table)
    out_ref[:, 2 * width :] = table.T.astype(BF)
    select_rows(experts, where_ref, out_ref, outs)


def route(where, ids_t, gates_t, hidden_in, out_grad, experts, count, size):
    tokens, width = hidden_in.shape
    wide = 2 * width + LANES
    block = jax.ShapeDtypeStruct((size, wide), BF)
    outs = pl.pallas_call(
        functools.partial(route_kernel, experts),
        in_specs=[IN_SMEM] + [IN_HBM] * 4,
        out_specs=[IN_VMEM] * (1 + count),
        out_shape=[jax.ShapeDtypeStruct((tokens, wide), BF)] + [block] * count,
        scratch_shapes=[
            pltpu.VMEM(ids_t.shape, ids_t.dtype),
            pltpu.VMEM(gates_t.shape, gates_t.dtype),
            pltpu.SemaphoreType.DMA((4,)),
        ],
        compiler_params=params(8),
        cost_estimate=CHEAP,
        name="route",
    )(where, *[remote(array) for array in (ids_t, gates_t, hidden_in, out_grad)])
    return outs[0], list(outs[1:])


def relay_kernel(in_ref, out_ref):
    out_ref[...] = in_ref[...]


def relay(array, deps):
    return call(
        relay_kernel,
        deps,
        [array],
        [IN_VMEM],
        out_specs=IN_VMEM,
        out_shape=jax.ShapeDtypeStruct(array.shape, array.dtype),
        compiler_params=params(4),
        cost_estimate=CHEAP,
        name="relay",
    )


def unpack_kernel(where_ref, groups_ref, ids_ref, *refs):
    blocks, (grad_ref, gate_ref, rows, place_ref, sems) = refs[:-5], refs[-5:]
    size = blocks[0].shape[0]
    tokens, width = grad_ref.shape
    me, flip = where_ref[0], where_ref[1]
    peers = me ^ lax.broadcasted_iota(jnp.int32, place_ref.shape, 0)
    member = jnp.zeros(place_ref.shape, F32)
    for index in range(groups_ref.shape[0]):
        member = jnp.where(groups_ref[index : index + 1, :] == peers, 1.0, member)
    earlier = jnp.where(
        lax.broadcasted_iota(jnp.int32, (tokens, tokens), 0)
        < lax.broadcasted_iota(jnp.int32, (tokens, tokens), 1),
        1.0,
        0.0,
    ).astype(BF)
    rank = dot_nn(member.astype(BF), earlier).astype(jnp.int32)
    place_ref[...] = jnp.where(member > 0.0, rank ^ flip, -1)
    pieces = [rows.at[index * size : (index + 1) * size] for index in range(len(blocks))]
    fetch(list(zip(blocks, pieces)), sems)
    hot = join([hot_block(place_ref, index, size) for index in range(len(blocks))])
    contract = (((0,), (0,)), ((), ()))
    grad_ref[...] = lax.dot_general(
        hot, rows[:, :width], contract, preferred_element_type=F32
    ).astype(BF)
    terms = lax.dot_general(rows[:, width:], hot, contract, preferred_element_type=F32)
    expert = lax.broadcasted_iota(jnp.int32, (LANES, tokens), 0)
    for index in range(ids_ref.shape[0]):
        chosen = jnp.where(ids_ref[index : index + 1, :] == expert, terms, 0.0)
        gate_ref[index : index + 1, :] = jnp.sum(chosen, axis=0, keepdims=True)


def unpack(where, groups_t, ids_t, blocks):
    size, wide = blocks[0].shape
    count, tokens = ids_t.shape
    return pl.pallas_call(
        unpack_kernel,
        in_specs=[IN_SMEM, IN_VMEM, IN_VMEM] + [ANYWHERE] * len(blocks),
        out_specs=[IN_VMEM] * 2,
        out_shape=[
            jax.ShapeDtypeStruct((tokens, wide - LANES), BF),
            jax.ShapeDtypeStruct((count, tokens), F32),
        ],
        scratch_shapes=[
            pltpu.VMEM((size * len(blocks), wide), BF),
            pltpu.VMEM((len(blocks), tokens), jnp.int32),
            pltpu.SemaphoreType.DMA((len(blocks),)),
        ],
        compiler_params=params(12),
        cost_estimate=CHEAP,
        name="unpack",
    )(where, groups_t, ids_t, *blocks)


def project_kernel(counts, starts, *refs):
    blocks = sum(counts)
    mats, (own_ref, other_ref, rows_ref, sems) = list(refs[blocks:-4]), refs[-4:]
    width = rows_ref.shape[2]
    half = refs[0].shape[0] // 2
    experts, _, kept, hid = own_ref.shape
    pairs, first = [], 0
    for which, (count, start) in enumerate(zip(counts, starts)):
        for index in range(count):
            for place in range(2):
                row = place * kept + index * half
                pairs.append(
                    (
                        refs[first + index].at[
                            place * half : (place + 1) * half, start : start + width
                        ],
                        rows_ref.at[which, row : row + half],
                    )
                )
        first += count
    fetch(pairs, sems)
    tile = tile_of(hid, 512)
    for e in range(experts):
        for begin in range(0, hid, tile):
            part = slice(begin, begin + tile)
            for index, mat in enumerate(mats):
                if index == len(mats) - 1 and len(mats) % 2:
                    value = dot_nt(rows_ref[len(counts) - 1], mat[e, part])
                else:
                    value = dot_nn(rows_ref[0], mat[e, :, part])
                own_ref[e, index, :, part] = value[:kept]
                other_ref[e, index, :, part] = value[kept:]


def project(pieces, mats, hid, width, deps):
    experts = mats[0].shape[0]
    blocks = [block for piece, _ in pieces for block in piece]
    kept = len(pieces[0][0]) * blocks[0].shape[0] // 2
    shape = jax.ShapeDtypeStruct((experts, len(mats), kept, hid), F32)
    counts, starts = [len(piece) for piece, _ in pieces], [start for _, start in pieces]
    return call(
        functools.partial(project_kernel, counts, starts),
        deps,
        [*blocks, *[resident(mat) for mat in mats]],
        [ANYWHERE] * len(blocks) + [IN_VMEM] * len(mats),
        out_specs=[IN_VMEM, IN_VMEM],
        out_shape=[shape, shape],
        scratch_shapes=[
            pltpu.VMEM((len(pieces), 2 * kept, width), BF),
            pltpu.SemaphoreType.DMA((2 * len(blocks),)),
        ],
        compiler_params=params(12),
        cost_estimate=CHEAP,
        name="project",
    )


def add_kernel(own_ref, other_ref, out_ref):
    experts, count, kept, _ = out_ref.shape
    for e in range(experts):
        for index in range(count):

            @pl.loop(0, kept // 16)
            def _(step):
                rows = pl.ds(pl.multiple_of(step * 16, 16), 16)
                total = own_ref[e, index, rows] + other_ref[e, index, rows]
                out_ref[e, index, rows] = total.astype(BF)


def add(own, other, deps):
    return call(
        add_kernel,
        deps,
        [own, other],
        [IN_VMEM] * 2,
        out_specs=IN_VMEM,
        out_shape=jax.ShapeDtypeStruct(own.shape, BF),
        compiler_params=params(12),
        cost_estimate=CHEAP,
        name="add",
    )


def act_kernel(blocks, pairs, where_ref, *refs):
    sums, refs = refs[: 2 * pairs], refs[2 * pairs :]
    acts_ref, gates_ref, sems = refs[blocks:]
    experts, _, kept, hid = sums[0].shape
    half = refs[0].shape[0] // 2
    width = refs[0].shape[1] - LANES
    fetch(
        [
            (block.at[:half, width:], gates_ref.at[index * half : (index + 1) * half])
            for index, block in enumerate(refs[:blocks])
        ],
        sems,
    )
    grad_at = 2 if pairs == 1 else 0
    tile = 16
    lane = lax.broadcasted_iota(jnp.int32, (tile, LANES), 1)
    for e in range(experts):
        mine = lane == where_ref[0] * experts + e

        @pl.loop(0, kept // tile)
        def _(step):
            rows = pl.ds(pl.multiple_of(step * tile, tile), tile)

            def both(pair, index):
                return pair[0][e, index, rows].astype(F32) + pair[1][e, index, rows].astype(F32)

            gates = gates_ref[rows].astype(F32)
            gate = jnp.sum(jnp.where(mine, gates, 0.0), axis=1, keepdims=True)
            pre_gate, pre_up = both(sums[:2], 0), both(sums[:2], 1)
            back = both(sums[-2:], grad_at)
            sig = jax.nn.sigmoid(pre_gate)
            silu = pre_gate * sig
            hidden = silu * pre_up
            grad_hidden = gate * back
            slope = sig * (1.0 + pre_gate * (1.0 - sig))
            acts_ref[e, rows, :hid] = (grad_hidden * pre_up * slope).astype(BF)
            acts_ref[e, rows, hid : 2 * hid] = (grad_hidden * silu).astype(BF)
            acts_ref[e, rows, 2 * hid : 3 * hid] = (gate * hidden).astype(BF)
            term = jnp.sum(hidden.astype(BF).astype(F32) * back, axis=1, keepdims=True)
            acts_ref[e, rows, 3 * hid :] = jnp.where(mine, term, 0.0).astype(BF)


def activate(where, sums, blocks, deps):
    experts, _, kept, hid = sums[0].shape
    return call(
        functools.partial(act_kernel, len(blocks), len(sums) // 2),
        deps,
        [where, *sums, *blocks],
        [IN_SMEM] + [IN_VMEM] * len(sums) + [ANYWHERE] * len(blocks),
        out_specs=IN_VMEM,
        out_shape=jax.ShapeDtypeStruct((experts, kept, 3 * hid + LANES), BF),
        scratch_shapes=[
            pltpu.VMEM((kept, LANES), BF),
            pltpu.SemaphoreType.DMA((len(blocks),)),
        ],
        compiler_params=params(8),
        cost_estimate=CHEAP,
        name="activate",
    )


def back_kernel(own_ref, other_ref, gate_ref, up_ref, *refs):
    outs, (acts_ref, terms_ref, sems) = refs[:-3], refs[-3:]
    experts, kept, _ = own_ref.shape
    half = outs[0].shape[0] // 2
    _, width, hid = gate_ref.shape
    pairs = []
    for place, ref in enumerate((own_ref, other_ref)):
        rows = slice(place * kept, (place + 1) * kept)
        pairs.append((ref.at[:, :, : 2 * hid], acts_ref.at[:, rows]))
        pairs.append((ref.at[:, :, 3 * hid :], terms_ref.at[:, rows]))
    fetch(pairs, sems)
    terms = terms_ref[0]
    for e in range(1, experts):
        terms = terms + terms_ref[e]

    def put(value, part):
        for index, out in enumerate(outs):
            out[:half, part] = value[index * half : (index + 1) * half]
            out[half:, part] = value[kept + index * half : kept + (index + 1) * half]

    put(terms, slice(width, width + LANES))
    tile = tile_of(width, 256)
    for start in range(0, width, tile):
        part = slice(start, start + tile)
        total = jnp.zeros((2 * kept, tile), F32)
        for e in range(experts):
            total = total + dot_nt(acts_ref[e, :, :hid], gate_ref[e, part])
            total = total + dot_nt(acts_ref[e, :, hid:], up_ref[e, part])
        put(total.astype(BF), part)


def back(own, other, w_gate, w_up, blocks, deps):
    experts, kept, _ = own.shape
    _, width, hid = w_gate.shape
    shape = jax.ShapeDtypeStruct((2 * kept // blocks, width + LANES), BF)
    return call(
        back_kernel,
        deps,
        [own, other, resident(w_gate), resident(w_up)],
        [ANYWHERE] * 2 + [IN_VMEM] * 2,
        out_specs=[IN_VMEM] * blocks,
        out_shape=[shape] * blocks,
        scratch_shapes=[
            pltpu.VMEM((experts, 2 * kept, 2 * hid), BF),
            pltpu.VMEM((experts, 2 * kept, LANES), BF),
            pltpu.SemaphoreType.DMA((4,)),
        ],
        compiler_params=params(12),
        cost_estimate=CHEAP,
        name="back",
    )


def grads_kernel(groups, *refs):
    blocks = sum(groups)
    acts = refs[2 * blocks : -6]
    out_gate, out_up, out_down, gate_acts, up_acts, hidden_t = refs[-6:]
    experts, _, hid = gate_acts.shape

    @pl.when(pl.program_id(0) == 0)
    def _():
        for e in range(experts):
            first = 0
            for ref in acts:
                rows = slice(first, first + ref.shape[1])
                gate_acts[e, rows] = ref[e, :, :hid]
                up_acts[e, rows] = ref[e, :, hid : 2 * hid]
                hidden_t[e, :, rows] = ref[e, :, 2 * hid : 3 * hid].T
                first += ref.shape[1]

    def rows_of(ins):
        out, first = [], 0
        for count in groups:
            group = ins[first : first + count]
            half = group[0].shape[0] // 2
            out += [ref[:half] for ref in group] + [ref[half:] for ref in group]
            first += count
        return join(out)

    rows_t = rows_of(refs[:blocks]).T
    grads = rows_of(refs[blocks : 2 * blocks])
    for e in range(experts):
        out_gate[e] = dot_nn(rows_t, gate_acts[e]).astype(BF)
        out_up[e] = dot_nn(rows_t, up_acts[e]).astype(BF)
        out_down[e] = dot_nn(hidden_t[e], grads).astype(BF)


def weight_grads(ins, grads, starts, width, acts, groups, deps):
    size = ins[0].shape[0]
    experts = acts[0].shape[0]
    hid = (acts[0].shape[2] - LANES) // 3
    rows = size * len(ins)
    tile = tile_of(width, 256)

    def row_spec(start):
        return pl.BlockSpec((size, tile), lambda j: (0, start // tile + j))

    wide = pl.BlockSpec((experts, tile, hid), lambda j: (0, j, 0))
    down = pl.BlockSpec((experts, hid, tile), lambda j: (0, 0, j))
    wide_shape = jax.ShapeDtypeStruct((experts, width, hid), BF)
    return call(
        functools.partial(grads_kernel, groups),
        deps,
        [*ins, *grads, *acts],
        [row_spec(0) for _ in ins]
        + [row_spec(start) for start in starts]
        + [pl.BlockSpec(act.shape, lambda j: (0, 0, 0)) for act in acts],
        grid=(width // tile,),
        out_specs=[wide, wide, down],
        out_shape=[wide_shape, wide_shape, jax.ShapeDtypeStruct((experts, hid, width), BF)],
        scratch_shapes=[
            pltpu.VMEM((experts, rows, hid), BF),
            pltpu.VMEM((experts, rows, hid), BF),
            pltpu.VMEM((experts, hid, rows), BF),
        ],
        compiler_params=params(48),
        cost_estimate=CHEAP,
        name="weight_grads",
    )


def mark_kernel(out_ref):
    out_ref[...] = jnp.zeros(out_ref.shape, F32)


def mark(deps):
    return call(
        mark_kernel,
        deps,
        [],
        [],
        out_specs=IN_VMEM,
        out_shape=jax.ShapeDtypeStruct((8, LANES), F32),
        compiler_params=params(1),
        cost_estimate=MARK,
        name="mark",
    )


def local(
    hidden_in, out_grad, expert_ids, group_ids, expert_slot, gate_weight, w_gate, w_up, w_down
):
    nodes = lax.axis_size("node")
    shares = lax.axis_size("local")
    experts = w_gate.shape[0]
    capacity = 4 * hidden_in.shape[0] // nodes
    me = lax.axis_index("node")
    core = lax.axis_index("local") % 2
    where = jnp.stack([me, core * (capacity // 2)]).astype(jnp.int32)
    quarter = nodes // 4
    spans = [range(group * quarter, (group + 1) * quarter) for group in range(4)]
    own, near, mid, far = range(4)

    def swap(value, step):
        return lax.ppermute(value, "local", [(i, i ^ step) for i in range(shares)])

    def cross(value, mask):
        if mask == 0:
            return value
        return lax.ppermute(value, "node", [(i, i ^ mask) for i in range(nodes)])

    ids_t = expert_ids.T
    width, hid = w_gate.shape[1:]
    last = []

    def send(blocks, masks):
        return [cross(block, mask) for block, mask in zip(blocks, masks)]

    def select_step(group, whole):
        blocks = select(where, whole, experts, quarter, capacity, last)
        last[:] = [blocks[0]]
        rows[group] = send(blocks, spans[0])

    def pause(count):
        for _ in range(count):
            last[:] = [mark(last)]

    def project_step(pieces, mats):
        mine, other = project(pieces, mats, hid, width, last)
        last[:] = [mine]
        return mine, swap(other, 1)

    def sum_step(mine, other):
        total = add(mine, other, last)
        last[:] = [total]
        step = 2
        while 2 * step < shares:
            total = (total.astype(F32) + swap(total, step).astype(F32)).astype(BF)
            step *= 2
        return [total, swap(total, step)]

    def whole_project(group):
        return project_step([(rows[group], 0), (rows[group], width)], mats)

    def act_step(group):
        mine = activate(where, sums[group], rows[group], last)
        last[:] = [mine]
        acts[group] = mine, swap(mine, 1)

    def settle(arrays):
        last[:] = [mark([*last, *arrays])]

    def back_step(group):
        blocks = back(*acts[group], v_gate, v_up, len(spans[group]), last)
        last[:] = [blocks[0]]
        for mask, block in zip(spans[group], send(blocks, spans[group])):
            returned[mask] = block

    rows, sums, acts = [[None] * 4 for _ in range(3)]
    returned = [None] * nodes
    whole, blocks = route(
        where, ids_t, gate_weight.T, hidden_in, out_grad, experts, 2 * quarter, capacity
    )
    last[:] = [whole]
    rows[own] = send(blocks[:quarter], spans[own])
    rows[near] = send(blocks[quarter:], spans[near])
    mid_whole = cross(whole, 2 * quarter)
    far_whole = cross(mid_whole, quarter)
    mats = load((w_gate, w_up, w_down), last)
    v_gate, v_up, v_down = mats
    last[:] = [v_gate]

    parts = [None] * 4
    parts[own] = whole_project(own)
    pause(8)
    sums[own] = sum_step(*parts[own])
    parts[near] = whole_project(near)
    select_step(mid, mid_whole)
    pause(8)
    sums[near] = sum_step(*parts[near])
    act_step(own)
    parts[mid] = whole_project(mid)
    select_step(far, far_whole)
    pause(8)
    sums[mid] = sum_step(*parts[mid])
    act_step(near)
    back_step(own)
    parts[far] = whole_project(far)
    pause(8)
    act_step(mid)
    sums[far] = sum_step(*parts[far])
    back_step(near)
    back_step(mid)
    act_step(far)
    pause(8)
    back_step(far)

    blocks = [block for group in rows for block in group]
    grad_w_gate, grad_w_up, grad_w_down = weight_grads(
        blocks,
        blocks,
        [width] * nodes,
        width,
        [part for pair in acts for part in pair],
        [len(span) for span in spans],
        last,
    )
    grad_input, grad_gate = unpack(where, group_ids.T, ids_t, returned)
    return (grad_input, grad_gate.T.astype(BF), grad_w_gate, grad_w_up, grad_w_down)


def solution(mesh):
    return jax.shard_map(
        local,
        mesh=mesh,
        in_specs=(
            P("node", "local"),
            P("node", "local"),
            P("node", None),
            P("node", None),
            P("node", None),
            P("node", None),
            P("node", "local", None),
            P("node", "local", None),
            P("node", None, "local"),
        ),
        out_specs=(
            P("node", "local"),
            P("node", None),
            P("node", "local", None),
            P("node", "local", None),
            P("node", None, "local"),
        ),
        check_vma=False,
    )
```

```python
import functools

import jax
import jax.numpy as jnp
from jax import lax
from jax.experimental import pallas as pl
from jax.experimental.pallas import tpu as pltpu
from jax.sharding import PartitionSpec as P

BF = jnp.bfloat16
F32 = jnp.float32
MIB = 1024 * 1024
LANES = 128
IN_VMEM = pl.BlockSpec(memory_space=pltpu.VMEM)
IN_SMEM = pl.BlockSpec(memory_space=pltpu.SMEM)
IN_HBM = pl.BlockSpec(memory_space=pltpu.HBM)
ANYWHERE = pl.BlockSpec(memory_space=pl.ANY)
MARK = pl.CostEstimate(flops=4000000000, bytes_accessed=1024, transcendentals=0)
CHEAP = pl.CostEstimate(flops=1024, bytes_accessed=1024, transcendentals=0)


def params(mib):
    return pltpu.CompilerParams(vmem_limit_bytes=mib * MIB)


def call(kernel, deps, operands, in_specs, **settings):
    count, extra = len(operands), len(deps)

    def body(*refs):
        kernel(*refs[:count], *refs[count + extra :])

    return pl.pallas_call(body, in_specs=list(in_specs) + [ANYWHERE] * extra, **settings)(
        *operands, *deps
    )


def tile_of(size, want):
    tile = min(size, want)
    while size % tile:
        tile //= 2
    return tile


def dot_nn(left, right):
    return lax.dot_general(left, right, (((1,), (0,)), ((), ())), preferred_element_type=F32)


def dot_nt(left, right):
    return lax.dot_general(left, right, (((1,), (1,)), ((), ())), preferred_element_type=F32)


def resident(array):
    return pltpu.with_memory_space_constraint(array, pltpu.VMEM)


def remote(array):
    return pltpu.with_memory_space_constraint(array, pltpu.HBM)


def begin(pairs, sems):
    copies = [pltpu.make_async_copy(src, dst, sems.at[i]) for i, (src, dst) in enumerate(pairs)]
    for copy in copies:
        copy.start()
    return copies


def fetch(pairs, sems):
    for copy in begin(pairs, sems):
        copy.wait()


def join(pieces):
    return pieces[0] if len(pieces) == 1 else jnp.concatenate(pieces, axis=0)


def load_kernel(count, *refs):
    fetch(list(zip(refs[:count], refs[count : 2 * count])), refs[2 * count])


def load(mats, deps):
    count = len(mats)
    return call(
        functools.partial(load_kernel, count),
        deps,
        [remote(mat) for mat in mats],
        [IN_HBM] * count,
        out_specs=[IN_VMEM] * count,
        out_shape=[pltpu.VMEM(mat.shape, mat.dtype) for mat in mats],
        scratch_shapes=[pltpu.SemaphoreType.DMA((count,))],
        compiler_params=params(1),
        cost_estimate=CHEAP,
        name="load",
    )


def hot_block(place_ref, index, size):
    tokens = place_ref.shape[1]
    row = lax.broadcasted_iota(jnp.int32, (size, tokens), 0)
    return jnp.where(place_ref[index : index + 1, :] == row, 1.0, 0.0).astype(BF)


def select_rows(experts, where_ref, tokens_ref, outs):
    me, flip = where_ref[0], where_ref[1]
    tokens, width = tokens_ref.shape
    size = outs[0].shape[0]
    lane = lax.broadcasted_iota(jnp.int32, (tokens, LANES), 1)
    holds = (
        lax.broadcasted_iota(jnp.int32, (LANES, LANES), 0) // experts
        == lax.broadcasted_iota(jnp.int32, (LANES, LANES), 1)
    )
    named = jnp.where(tokens_ref[:, width - LANES :].astype(F32) > 0.0, 1.0, 0.0).astype(BF)
    member = dot_nn(named, jnp.where(holds, 1.0, 0.0).astype(BF)) > 0.0
    earlier = (
        lax.broadcasted_iota(jnp.int32, (tokens, tokens), 1)
        < lax.broadcasted_iota(jnp.int32, (tokens, tokens), 0)
    )
    rank = dot_nn(
        jnp.where(earlier, 1.0, 0.0).astype(BF), jnp.where(member, 1.0, 0.0).astype(BF)
    )
    place = jnp.where(member, rank.astype(jnp.int32) ^ flip, -1)
    contract = (((0,), (0,)), ((), ()))
    for index, out in enumerate(outs):
        row = jnp.sum(jnp.where(lane == (me ^ index), place, 0), axis=1, keepdims=True)
        hot = lax.broadcasted_iota(jnp.int32, (tokens, size), 1) == row
        hot = jnp.where(hot, 1.0, 0.0).astype(BF)
        out[...] = lax.dot_general(
            hot, tokens_ref[...], contract, preferred_element_type=F32
        ).astype(BF)


def select_kernel(experts, where_ref, tokens_ref, *outs):
    select_rows(experts, where_ref, tokens_ref, outs)


def select(where, whole, experts, count, size, deps):
    block = jax.ShapeDtypeStruct((size, whole.shape[1]), BF)
    return call(
        functools.partial(select_kernel, experts),
        deps,
        [where, whole],
        [IN_SMEM, IN_VMEM],
        out_specs=[IN_VMEM] * count,
        out_shape=[block] * count,
        compiler_params=params(8),
        cost_estimate=CHEAP,
        name="select",
    )


def route_kernel(experts, where_ref, ids_hbm, gates_hbm, in_hbm, grad_hbm, *refs):
    out_ref, outs = refs[0], refs[1:-3]
    ids_ref, gates_ref, sems = refs[-3:]
    tokens, width = in_hbm.shape
    fetch(
        [
            (ids_hbm, ids_ref),
            (gates_hbm, gates_ref),
            (in_hbm, out_ref.at[:, :width]),
            (grad_hbm, out_ref.at[:, width : 2 * width]),
        ],
        sems,
    )
    expert = lax.broadcasted_iota(jnp.int32, (LANES, tokens), 0)
    table = jnp.zeros((LANES, tokens), F32)
    for index in range(ids_ref.shape[0]):
        gate = gates_ref[index : index + 1, :].astype(F32)
        table = jnp.where(ids_ref[index : index + 1, :] == expert, gate, table)
    out_ref[:, 2 * width :] = table.T.astype(BF)
    select_rows(experts, where_ref, out_ref, outs)


def route(where, ids_t, gates_t, hidden_in, out_grad, experts, count, size):
    tokens, width = hidden_in.shape
    wide = 2 * width + LANES
    block = jax.ShapeDtypeStruct((size, wide), BF)
    outs = pl.pallas_call(
        functools.partial(route_kernel, experts),
        in_specs=[IN_SMEM] + [IN_HBM] * 4,
        out_specs=[IN_VMEM] * (1 + count),
        out_shape=[jax.ShapeDtypeStruct((tokens, wide), BF)] + [block] * count,
        scratch_shapes=[
            pltpu.VMEM(ids_t.shape, ids_t.dtype),
            pltpu.VMEM(gates_t.shape, gates_t.dtype),
            pltpu.SemaphoreType.DMA((4,)),
        ],
        compiler_params=params(8),
        cost_estimate=CHEAP,
        name="route",
    )(where, *[remote(array) for array in (ids_t, gates_t, hidden_in, out_grad)])
    return outs[0], list(outs[1:])


def unpack_kernel(where_ref, groups_ref, ids_ref, *refs):
    blocks, (grad_ref, gate_ref, rows, place_ref, sems) = refs[:-5], refs[-5:]
    size = blocks[0].shape[0]
    tokens, width = grad_ref.shape
    pieces = [rows.at[index * size : (index + 1) * size] for index in range(len(blocks))]
    copies = begin(list(zip(blocks, pieces)), sems)
    me, flip = where_ref[0], where_ref[1]
    peers = me ^ lax.broadcasted_iota(jnp.int32, place_ref.shape, 0)
    member = jnp.zeros(place_ref.shape, F32)
    for index in range(groups_ref.shape[0]):
        member = jnp.where(groups_ref[index : index + 1, :] == peers, 1.0, member)
    earlier = jnp.where(
        lax.broadcasted_iota(jnp.int32, (tokens, tokens), 0)
        < lax.broadcasted_iota(jnp.int32, (tokens, tokens), 1),
        1.0,
        0.0,
    ).astype(BF)
    rank = dot_nn(member.astype(BF), earlier).astype(jnp.int32)
    place_ref[...] = jnp.where(member > 0.0, rank ^ flip, -1)
    hot = join([hot_block(place_ref, index, size) for index in range(len(blocks))])
    hot_t = hot.T
    for copy in copies:
        copy.wait()
    grad_ref[...] = dot_nn(hot_t, rows[:, :width]).astype(BF)
    terms = lax.dot_general(
        rows[:, width:], hot, (((0,), (0,)), ((), ())), preferred_element_type=F32
    )
    expert = lax.broadcasted_iota(jnp.int32, (LANES, tokens), 0)
    for index in range(ids_ref.shape[0]):
        chosen = jnp.where(ids_ref[index : index + 1, :] == expert, terms, 0.0)
        gate_ref[index : index + 1, :] = jnp.sum(chosen, axis=0, keepdims=True)


def unpack(where, groups_t, ids_t, blocks):
    size, wide = blocks[0].shape
    count, tokens = ids_t.shape
    return pl.pallas_call(
        unpack_kernel,
        in_specs=[IN_SMEM, IN_VMEM, IN_VMEM] + [ANYWHERE] * len(blocks),
        out_specs=[IN_VMEM] * 2,
        out_shape=[
            jax.ShapeDtypeStruct((tokens, wide - LANES), BF),
            jax.ShapeDtypeStruct((count, tokens), F32),
        ],
        scratch_shapes=[
            pltpu.VMEM((size * len(blocks), wide), BF),
            pltpu.VMEM((len(blocks), tokens), jnp.int32),
            pltpu.SemaphoreType.DMA((len(blocks),)),
        ],
        compiler_params=params(12),
        cost_estimate=CHEAP,
        name="unpack",
    )(where, groups_t, ids_t, *blocks)


def project_kernel(counts, starts, *refs):
    blocks = sum(counts)
    mats, (own_ref, other_ref, rows_ref, sems) = list(refs[blocks:-4]), refs[-4:]
    width = rows_ref.shape[2]
    half = refs[0].shape[0] // 2
    experts, _, kept, hid = own_ref.shape
    pairs, first = [], 0
    for which, (count, start) in enumerate(zip(counts, starts)):
        for index in range(count):
            for place in range(2):
                row = place * kept + index * half
                pairs.append(
                    (
                        refs[first + index].at[
                            place * half : (place + 1) * half, start : start + width
                        ],
                        rows_ref.at[which, row : row + half],
                    )
                )
        first += count
    fetch(pairs, sems)
    tile = tile_of(hid, 512)
    for e in range(experts):
        for begin in range(0, hid, tile):
            part = slice(begin, begin + tile)
            for index, mat in enumerate(mats):
                if index == len(mats) - 1 and len(mats) % 2:
                    value = dot_nt(rows_ref[len(counts) - 1], mat[e, part])
                else:
                    value = dot_nn(rows_ref[0], mat[e, :, part])
                own_ref[e, index, :, part] = value[:kept]
                other_ref[e, index, :, part] = value[kept:]


def project(pieces, mats, hid, width, deps):
    experts = mats[0].shape[0]
    blocks = [block for piece, _ in pieces for block in piece]
    kept = len(pieces[0][0]) * blocks[0].shape[0] // 2
    shape = jax.ShapeDtypeStruct((experts, len(mats), kept, hid), F32)
    counts, starts = [len(piece) for piece, _ in pieces], [start for _, start in pieces]
    return call(
        functools.partial(project_kernel, counts, starts),
        deps,
        [*blocks, *[resident(mat) for mat in mats]],
        [ANYWHERE] * len(blocks) + [IN_VMEM] * len(mats),
        out_specs=[IN_VMEM, IN_VMEM],
        out_shape=[shape, shape],
        scratch_shapes=[
            pltpu.VMEM((len(pieces), 2 * kept, width), BF),
            pltpu.SemaphoreType.DMA((2 * len(blocks),)),
        ],
        compiler_params=params(12),
        cost_estimate=CHEAP,
        name="project",
    )


def add_kernel(own_ref, other_ref, out_ref):
    experts, count, kept, _ = out_ref.shape
    for e in range(experts):
        for index in range(count):

            @pl.loop(0, kept // 16)
            def _(step):
                rows = pl.ds(pl.multiple_of(step * 16, 16), 16)
                total = own_ref[e, index, rows] + other_ref[e, index, rows]
                out_ref[e, index, rows] = total.astype(BF)


def add(own, other, deps):
    return call(
        add_kernel,
        deps,
        [own, other],
        [IN_VMEM] * 2,
        out_specs=IN_VMEM,
        out_shape=jax.ShapeDtypeStruct(own.shape, BF),
        compiler_params=params(12),
        cost_estimate=CHEAP,
        name="add",
    )


def act_kernel(blocks, pairs, where_ref, *refs):
    sums, refs = refs[: 2 * pairs], refs[2 * pairs :]
    acts_ref, gates_ref, sems = refs[blocks:]
    experts, _, kept, hid = sums[0].shape
    half = refs[0].shape[0] // 2
    width = refs[0].shape[1] - LANES
    fetch(
        [
            (block.at[:half, width:], gates_ref.at[index * half : (index + 1) * half])
            for index, block in enumerate(refs[:blocks])
        ],
        sems,
    )
    grad_at = 2 if pairs == 1 else 0
    tile = 16
    lane = lax.broadcasted_iota(jnp.int32, (tile, LANES), 1)
    for e in range(experts):
        mine = lane == where_ref[0] * experts + e

        @pl.loop(0, kept // tile)
        def _(step):
            rows = pl.ds(pl.multiple_of(step * tile, tile), tile)

            def both(pair, index):
                return pair[0][e, index, rows].astype(F32) + pair[1][e, index, rows].astype(F32)

            gates = gates_ref[rows].astype(F32)
            gate = jnp.sum(jnp.where(mine, gates, 0.0), axis=1, keepdims=True)
            pre_gate, pre_up = both(sums[:2], 0), both(sums[:2], 1)
            back = both(sums[-2:], grad_at)
            sig = jax.nn.sigmoid(pre_gate)
            silu = pre_gate * sig
            hidden = silu * pre_up
            grad_hidden = gate * back
            slope = sig * (1.0 + pre_gate * (1.0 - sig))
            acts_ref[e, rows, :hid] = (grad_hidden * pre_up * slope).astype(BF)
            acts_ref[e, rows, hid : 2 * hid] = (grad_hidden * silu).astype(BF)
            acts_ref[e, rows, 2 * hid : 3 * hid] = (gate * hidden).astype(BF)
            term = jnp.sum(hidden.astype(BF).astype(F32) * back, axis=1, keepdims=True)
            acts_ref[e, rows, 3 * hid :] = jnp.where(mine, term, 0.0).astype(BF)


def activate(where, sums, blocks, deps):
    experts, _, kept, hid = sums[0].shape
    return call(
        functools.partial(act_kernel, len(blocks), len(sums) // 2),
        deps,
        [where, *sums, *blocks],
        [IN_SMEM] + [IN_VMEM] * len(sums) + [ANYWHERE] * len(blocks),
        out_specs=IN_VMEM,
        out_shape=jax.ShapeDtypeStruct((experts, kept, 3 * hid + LANES), BF),
        scratch_shapes=[
            pltpu.VMEM((kept, LANES), BF),
            pltpu.SemaphoreType.DMA((len(blocks),)),
        ],
        compiler_params=params(8),
        cost_estimate=CHEAP,
        name="activate",
    )


def back_kernel(own_ref, other_ref, gate_ref, up_ref, *refs):
    outs, (acts_ref, terms_ref, sems) = refs[:-3], refs[-3:]
    experts, kept, _ = own_ref.shape
    half = outs[0].shape[0] // 2
    _, width, hid = gate_ref.shape
    pairs = []
    for place, ref in enumerate((own_ref, other_ref)):
        rows = slice(place * kept, (place + 1) * kept)
        pairs.append((ref.at[:, :, : 2 * hid], acts_ref.at[:, rows]))
        pairs.append((ref.at[:, :, 3 * hid :], terms_ref.at[:, rows]))
    fetch(pairs, sems)
    terms = terms_ref[0]
    for e in range(1, experts):
        terms = terms + terms_ref[e]

    def put(value, part):
        for index, out in enumerate(outs):
            out[:half, part] = value[index * half : (index + 1) * half]
            out[half:, part] = value[kept + index * half : kept + (index + 1) * half]

    put(terms, slice(width, width + LANES))
    tile = tile_of(width, 256)
    for start in range(0, width, tile):
        part = slice(start, start + tile)
        total = jnp.zeros((2 * kept, tile), F32)
        for e in range(experts):
            total = total + dot_nt(acts_ref[e, :, :hid], gate_ref[e, part])
            total = total + dot_nt(acts_ref[e, :, hid:], up_ref[e, part])
        put(total.astype(BF), part)


def back(own, other, w_gate, w_up, blocks, deps):
    experts, kept, _ = own.shape
    _, width, hid = w_gate.shape
    shape = jax.ShapeDtypeStruct((2 * kept // blocks, width + LANES), BF)
    return call(
        back_kernel,
        deps,
        [own, other, resident(w_gate), resident(w_up)],
        [ANYWHERE] * 2 + [IN_VMEM] * 2,
        out_specs=[IN_VMEM] * blocks,
        out_shape=[shape] * blocks,
        scratch_shapes=[
            pltpu.VMEM((experts, 2 * kept, 2 * hid), BF),
            pltpu.VMEM((experts, 2 * kept, LANES), BF),
            pltpu.SemaphoreType.DMA((4,)),
        ],
        compiler_params=params(12),
        cost_estimate=CHEAP,
        name="back",
    )


def gather_kernel(groups, *refs):
    blocks = sum(groups)
    acts = refs[blocks:-7]
    rows_t, grads, gate_acts, up_acts, hidden_t, rows_ref, sems = refs[-7:]
    width, hid = rows_t.shape[0], gate_acts.shape[2]
    pairs, first, row = [], 0, 0
    for count in groups:
        half = refs[first].shape[0] // 2
        for place in range(2):
            for index in range(count):
                block = refs[first + index].at[place * half : (place + 1) * half]
                pairs.append((block.at[:, :width], rows_ref.at[row : row + half]))
                pairs.append((block.at[:, width : 2 * width], grads.at[row : row + half]))
                row += half
        first += count
    copies = begin(pairs, sems)
    for e in range(gate_acts.shape[0]):
        row = 0
        for ref in acts:
            rows = slice(row, row + ref.shape[1])
            gate_acts[e, rows] = ref[e, :, :hid]
            up_acts[e, rows] = ref[e, :, hid : 2 * hid]
            hidden_t[e, :, rows] = ref[e, :, 2 * hid : 3 * hid].T
            row += ref.shape[1]
    for copy in copies:
        copy.wait()
    rows_t[...] = rows_ref[...].T


def gather_rows(blocks, acts, groups, width, deps):
    size = blocks[0].shape[0]
    experts = acts[0].shape[0]
    hid = (acts[0].shape[2] - LANES) // 3
    rows = size * len(blocks)
    return call(
        functools.partial(gather_kernel, groups),
        deps,
        [*blocks, *acts],
        [ANYWHERE] * len(blocks) + [IN_VMEM] * len(acts),
        out_specs=[IN_VMEM] * 5,
        out_shape=[
            jax.ShapeDtypeStruct((width, rows), BF),
            jax.ShapeDtypeStruct((rows, width), BF),
            jax.ShapeDtypeStruct((experts, rows, hid), BF),
            jax.ShapeDtypeStruct((experts, rows, hid), BF),
            jax.ShapeDtypeStruct((experts, hid, rows), BF),
        ],
        scratch_shapes=[
            pltpu.VMEM((rows, width), BF),
            pltpu.SemaphoreType.DMA((4 * len(blocks),)),
        ],
        compiler_params=params(20),
        cost_estimate=CHEAP,
        name="gather_rows",
    )


def grads_kernel(groups, first_t, first_grads, first_gate, first_up, first_hidden, *refs):
    blocks = sum(groups)
    acts = refs[2 * blocks : -6]
    out_gate, out_up, out_down, gate_acts, up_acts, hidden_t = refs[-6:]
    experts, _, hid = gate_acts.shape

    @pl.when(pl.program_id(0) == 0)
    def _():
        for e in range(experts):
            first = 0
            for ref in acts:
                rows = slice(first, first + ref.shape[1])
                gate_acts[e, rows] = ref[e, :, :hid]
                up_acts[e, rows] = ref[e, :, hid : 2 * hid]
                hidden_t[e, :, rows] = ref[e, :, 2 * hid : 3 * hid].T
                first += ref.shape[1]

    def rows_of(ins):
        out, first = [], 0
        for count in groups:
            group = ins[first : first + count]
            half = group[0].shape[0] // 2
            out += [ref[:half] for ref in group] + [ref[half:] for ref in group]
            first += count
        return join(out)

    rows_t = rows_of(refs[:blocks]).T
    grads = rows_of(refs[blocks : 2 * blocks])
    for e in range(experts):
        gate = dot_nn(first_t[...], first_gate[e]) + dot_nn(rows_t, gate_acts[e])
        out_gate[e] = gate.astype(BF)
        up = dot_nn(first_t[...], first_up[e]) + dot_nn(rows_t, up_acts[e])
        out_up[e] = up.astype(BF)
        down = dot_nn(first_hidden[e], first_grads[...]) + dot_nn(hidden_t[e], grads)
        out_down[e] = down.astype(BF)


def weight_grads(gathered, blocks, acts, groups, width, deps):
    size = blocks[0].shape[0]
    experts = acts[0].shape[0]
    hid = (acts[0].shape[2] - LANES) // 3
    rows = size * len(blocks)
    tile = tile_of(width, 256)
    steps = width // tile
    before = gathered[1].shape[0]

    def fixed(array):
        return pl.BlockSpec(array.shape, lambda j: (0, 0, 0))

    wide = pl.BlockSpec((experts, tile, hid), lambda j: (0, j, 0))
    down = pl.BlockSpec((experts, hid, tile), lambda j: (0, 0, j))
    wide_shape = jax.ShapeDtypeStruct((experts, width, hid), BF)
    return call(
        functools.partial(grads_kernel, groups),
        deps,
        [*gathered, *blocks, *blocks, *acts],
        [
            pl.BlockSpec((tile, before), lambda j: (j, 0)),
            pl.BlockSpec((before, tile), lambda j: (0, j)),
            *[fixed(array) for array in gathered[2:]],
        ]
        + [pl.BlockSpec((size, tile), lambda j: (0, j)) for _ in blocks]
        + [pl.BlockSpec((size, tile), lambda j: (0, steps + j)) for _ in blocks]
        + [fixed(act) for act in acts],
        grid=(steps,),
        out_specs=[wide, wide, down],
        out_shape=[wide_shape, wide_shape, jax.ShapeDtypeStruct((experts, hid, width), BF)],
        scratch_shapes=[
            pltpu.VMEM((experts, rows, hid), BF),
            pltpu.VMEM((experts, rows, hid), BF),
            pltpu.VMEM((experts, hid, rows), BF),
        ],
        compiler_params=params(48),
        cost_estimate=CHEAP,
        name="weight_grads",
    )


def mark_kernel(out_ref):
    out_ref[...] = jnp.zeros(out_ref.shape, F32)


def mark(deps):
    return call(
        mark_kernel,
        deps,
        [],
        [],
        out_specs=IN_VMEM,
        out_shape=jax.ShapeDtypeStruct((8, LANES), F32),
        compiler_params=params(1),
        cost_estimate=MARK,
        name="mark",
    )


def local(
    hidden_in, out_grad, expert_ids, group_ids, expert_slot, gate_weight, w_gate, w_up, w_down
):
    nodes = lax.axis_size("node")
    shares = lax.axis_size("local")
    experts = w_gate.shape[0]
    capacity = 4 * hidden_in.shape[0] // nodes
    me = lax.axis_index("node")
    core = lax.axis_index("local") % 2
    where = jnp.stack([me, core * (capacity // 2)]).astype(jnp.int32)
    quarter = nodes // 4
    cuts = [0, quarter, 2 * quarter, 3 * quarter, nodes]
    spans = [range(start, end) for start, end in zip(cuts, cuts[1:])]
    own, near, mid, far = range(4)

    def swap(value, step):
        return lax.ppermute(value, "local", [(i, i ^ step) for i in range(shares)])

    def cross(value, mask):
        if mask == 0:
            return value
        return lax.ppermute(value, "node", [(i, i ^ mask) for i in range(nodes)])

    ids_t = expert_ids.T
    width, hid = w_gate.shape[1:]
    last = []

    def send(blocks, masks):
        return [cross(block, mask) for block, mask in zip(blocks, masks)]

    def select_step():
        blocks = select(where, mid_whole, experts, 2 * quarter, capacity, last)
        last[:] = [blocks[0]]
        rows[mid] = send(blocks[:quarter], spans[own])
        passed = send(blocks[quarter:], spans[near])
        for group in range(far, len(spans)):
            first = 3 * quarter
            rows[group] = passed[spans[group][0] - first : spans[group][-1] + 1 - first]

    def pause(count):
        for _ in range(count):
            last[:] = [mark(last)]

    def project_step(pieces, mats):
        mine, other = project(pieces, mats, hid, width, last)
        last[:] = [mine]
        return mine, swap(other, 1)

    def sum_step(mine, other):
        total = add(mine, other, last)
        last[:] = [total]
        step = 2
        while 2 * step < shares:
            total = (total.astype(F32) + swap(total, step).astype(F32)).astype(BF)
            step *= 2
        return [total, swap(total, step)]

    def whole_project(group):
        return project_step([(rows[group], 0), (rows[group], width)], mats)

    def act_step(group):
        mine = activate(where, sums[group], rows[group], last)
        last[:] = [mine]
        acts[group] = mine, swap(mine, 1)

    def settle(arrays):
        last[:] = [mark([*last, *arrays])]

    def gather_step():
        blocks = [block for group in rows[:2] for block in group]
        arrays = gather_rows(
            blocks,
            [part for pair in acts[:2] for part in pair],
            [len(span) for span in spans[:2]],
            width,
            last,
        )
        last[:] = [arrays[0]]
        return arrays

    def back_step(group):
        blocks = back(*acts[group], v_gate, v_up, len(spans[group]), last)
        last[:] = [blocks[0]]
        for mask, block in zip(spans[group], send(blocks, spans[group])):
            returned[mask] = block

    rows, sums, acts = [[None] * len(spans) for _ in range(3)]
    returned = [None] * nodes
    whole, blocks = route(
        where, ids_t, gate_weight.T, hidden_in, out_grad, experts, 2 * quarter, capacity
    )
    last[:] = [whole]
    rows[own] = send(blocks[:quarter], spans[own])
    rows[near] = send(blocks[quarter:], spans[near])
    mid_whole = cross(whole, 2 * quarter)
    mats = load((w_gate, w_up, w_down), last)
    v_gate, v_up, v_down = mats
    last[:] = [v_gate]

    parts = [None] * len(spans)
    parts[own] = whole_project(own)
    pause(8)
    sums[own] = sum_step(*parts[own])
    parts[near] = whole_project(near)
    select_step()
    pause(8)
    sums[near] = sum_step(*parts[near])
    act_step(own)
    parts[mid] = whole_project(mid)
    pause(8)
    sums[mid] = sum_step(*parts[mid])
    parts[far] = whole_project(far)
    act_step(near)
    back_step(own)
    pause(8)
    back_step(near)
    act_step(mid)
    sums[far] = sum_step(*parts[far])
    back_step(mid)
    gathered = gather_step()
    settle([returned[mask] for mask in spans[near]])
    act_step(far)
    pause(8)
    back_step(far)

    grad_w_gate, grad_w_up, grad_w_down = weight_grads(
        gathered,
        [block for group in rows[2:] for block in group],
        [part for pair in acts[2:] for part in pair],
        [len(span) for span in spans[2:]],
        width,
        last,
    )
    grad_input, grad_gate = unpack(where, group_ids.T, ids_t, returned)
    return (grad_input, grad_gate.T.astype(BF), grad_w_gate, grad_w_up, grad_w_down)


def solution(mesh):
    return jax.shard_map(
        local,
        mesh=mesh,
        in_specs=(
            P("node", "local"),
            P("node", "local"),
            P("node", None),
            P("node", None),
            P("node", None),
            P("node", None),
            P("node", "local", None),
            P("node", "local", None),
            P("node", None, "local"),
        ),
        out_specs=(
            P("node", "local"),
            P("node", None),
            P("node", "local", None),
            P("node", "local", None),
            P("node", None, "local"),
        ),
        check_vma=False,
    )
```
